256 devices in a mesh: lon: 16 (over x_hi, z), tp: 16 (over y, x_lo, core).
Axes of the slice: x: 4 (x_hi: 2, x_lo: 2; x = x_hi * 2 + x_lo), y: 4, z: 8, core: 2. Of those that a mesh axis runs over, the one named last changes fastest.
Arguments:
- activations: bfloat16 [384, 2, 12, 1024], P('lon'), may hold values from -6 to 6
- qkv_weight: bfloat16 [3, 1024, 1024], P(None, None, 'tp'), may hold values from -0.1875 to 0.1875
- proj_weight: bfloat16 [1024, 1024], P('tp'), may hold values from -0.1875 to 0.1875
- pos_bias: float32 [16, 144, 144], P('tp'), may hold values from -3 to 302
- out_grad: bfloat16 [384, 2, 12, 1024], P('lon', None, None, 'tp'), may hold values from -6 to 6
Outputs:
- in_grad: bfloat16 [384, 2, 12, 1024], P('lon', None, None, 'tp')
- qkv_grad: float32 [3, 1024, 1024], P(None, 'lon', 'tp')
- proj_grad: float32 [1024, 1024], P('tp', 'lon')
- bias_grad: float32 [16, 144, 144], P('tp', 'lon')
The draws below stay inside these ranges and needn't reach their ends.
All inputs are finite; a program needn't handle non-finite values.
Results may differ from the reference program's by a relative error of at most 0.019.
Values may be sent and summed in bfloat16 or wider, within the bound.
A program may use at most 384 MiB of HBM per device.

```python
import jax
import jax.numpy as jnp
from jax import lax

D = 1024
H = 16
WIN_LON = 12
CELLS = 12
ROWS = 2
HD = 64
WT = 144
NLON = 384


def draw_pos_bias(key, part):
    key = jax.random.fold_in(key, 7)
    shape_all = (H, WT, WT)
    base = 0.8 * jax.random.truncated_normal(key, -3.75, 3.75, shape_all, jnp.float32)
    return base


def level_of(stream_key, shape, pieces, low, largest):
    loudness, own = 1.0, jax.random.fold_in(stream_key, 6)
    for position, blocks in pieces:
        steps = jnp.exp(jax.random.uniform(jax.random.fold_in(own, position), (blocks,), jnp.float32, low / len(pieces), largest / len(pieces)))
        loudness = loudness * jnp.repeat(steps, shape[position] // blocks).reshape([-1 if axis == position else 1 for axis in range(len(shape))])
    return loudness


def bell_draw(own_key, extent, scale, limit, pieces=(), dtype=jnp.bfloat16):
    gain = level_of(own_key, extent, pieces, -0.22, 0.18) if pieces else 1.0
    result = jax.random.normal(own_key, extent, jnp.float32) * scale * gain
    return jnp.minimum(jnp.maximum(result, -limit), limit).astype(dtype)


def setup_inputs(seed: int = 0) -> dict:
    seeds = jax.random.split(jax.random.key(seed), 6)
    activations = bell_draw(seeds[0], (NLON, ROWS, CELLS, D), 1.0, 6.0, ((0, 16),))
    qkv_weight = bell_draw(seeds[1], (3, D, D), D ** -0.5, 0.1875, ((2, 16),))
    proj_weight = bell_draw(seeds[2], (D, D), D ** -0.5, 0.1875, ((0, 16),))
    pos_bias = draw_pos_bias(jax.random.fold_in(seeds[5], 71), 0)
    out_grad = bell_draw(seeds[4], (NLON, ROWS, CELLS, D), 1.0, 6.0, ((0, 16), (3, 16)))
    return dict(activations=activations, qkv_weight=qkv_weight, proj_weight=proj_weight, pos_bias=pos_bias, out_grad=out_grad)


def product(spec, left, right):
    return jnp.einsum(spec, left.astype(jnp.float32), right.astype(jnp.float32))

def to_windows(field):
    lon_len, rows, cells, width = field.shape
    count = lon_len // WIN_LON
    grouped = field.reshape(count, WIN_LON, rows, cells, width).transpose(0, 2, 1, 3, 4)
    return grouped.reshape(count * rows, WIN_LON * cells, width)

def from_windows(field, lon_len, rows, cells):
    count = lon_len // WIN_LON
    width = field.shape[-1]
    grouped = field.reshape(count, rows, WIN_LON, cells, width).transpose(0, 2, 1, 3, 4)
    return grouped.reshape(lon_len, rows, cells, width)

def reference(activations, qkv_weight, proj_weight, pos_bias, out_grad):
    half_win = WIN_LON // 2
    att_scale = 1.0 / jnp.sqrt(jnp.float32(HD))
    widened = activations.astype(jnp.float32)
    centered = widened - lax.optimization_barrier(jnp.mean(widened, axis=-1, keepdims=True))
    inv_dev = lax.rsqrt(lax.optimization_barrier(jnp.mean(centered * centered, axis=-1, keepdims=True)) + 1e-05)
    normed = centered * inv_dev
    shifted = jnp.roll(normed.astype(jnp.bfloat16), -half_win, axis=0)
    grad_shift = jnp.roll(out_grad, -half_win, axis=0)
    windows = to_windows(shifted)
    grad_win = to_windows(grad_shift)

    def one_window(pair):
        tokens_win, grads_win = pair
        qkv_all = product('td,cde->cte', tokens_win, qkv_weight).astype(jnp.bfloat16)
        query = qkv_all[0].reshape(WT, H, HD)
        key_part = qkv_all[1].reshape(WT, H, HD)
        value_part = qkv_all[2].reshape(WT, H, HD)
        scores = product('qhe,khe->hqk', query, key_part) * att_scale + pos_bias
        probs = jax.nn.softmax(scores, axis=-1)
        probs_low = probs.astype(jnp.bfloat16)
        attended = product('hqk,khe->qhe', probs_low, value_part).astype(jnp.bfloat16).reshape(WT, D)
        grad_attn = product('td,ed->te', grads_win, proj_weight).astype(jnp.bfloat16).reshape(WT, H, HD)
        grad_probs = product('qhe,khe->hqk', grad_attn, value_part)
        grad_scores = probs * (grad_probs - lax.optimization_barrier(jnp.sum(grad_probs * probs, axis=-1, keepdims=True)))
        grad_value = product('hqk,qhe->khe', probs_low, grad_attn).astype(jnp.bfloat16)
        grad_low = grad_scores.astype(jnp.bfloat16)
        grad_query = (product('hqk,khe->qhe', grad_low, key_part) * att_scale).astype(jnp.bfloat16)
        grad_key = (product('hqk,qhe->khe', grad_low, query) * att_scale).astype(jnp.bfloat16)
        grad_qkv = jnp.stack([grad_query, grad_key, grad_value]).reshape(3, WT, D)
        return (attended, grad_qkv, grad_scores)
    attended, grad_qkv, grad_scores = lax.map(one_window, (windows, grad_win))
    proj_grad = product('nte,ntd->ed', attended, grad_win)
    qkv_grad = product('ntd,ncte->cde', windows, grad_qkv)
    bias_grad = lax.optimization_barrier(jnp.sum(grad_scores, axis=0))
    grad_windows = product('ncte,cde->ntd', grad_qkv, qkv_weight)
    grad_shifted = from_windows(grad_windows, NLON, ROWS, CELLS)
    grad_normed = jnp.roll(grad_shifted, half_win, axis=0)
    first = lax.optimization_barrier(jnp.mean(grad_normed, axis=-1, keepdims=True))
    second = lax.optimization_barrier(jnp.mean(grad_normed * normed, axis=-1, keepdims=True))
    in_grad = (out_grad.astype(jnp.float32) + inv_dev * (grad_normed - first - normed * second)).astype(jnp.bfloat16)
    return (in_grad, qkv_grad, proj_grad, bias_grad)
```

```python
import functools

import jax
import jax.numpy as jnp
from jax import lax
from jax.experimental import pallas as pl
from jax.experimental.pallas import tpu as pltpu
from jax.sharding import PartitionSpec as P

BF = jnp.bfloat16
F32 = jnp.float32
MESH = pl.DeviceIdType.MESH

LON = 24
ROWS = 2
CELLS = 12
D = 1024
HD = 64
WT = 144
NT = 288
HALF = 72
HPAD = 80
CHIPS = 8
ZL = 8
SCALE = 0.125


def nt(a, b):
    return lax.dot_general(a, b, (((1,), (1,)), ((), ())), preferred_element_type=F32)


def tn(a, b):
    return lax.dot_general(a, b, (((0,), (0,)), ((), ())), preferred_element_type=F32)


def nn(a, b):
    return jnp.dot(a, b, preferred_element_type=F32)


def kernel(
    act,
    qw,
    pw,
    pb,
    og,
    out_in,
    out_qkv,
    out_proj,
    out_bias,
    act_v,
    og_v,
    qw_v,
    pw_v,
    pb_v,
    xs,
    hs,
    hsend,
    hrecv,
    nf,
    xb,
    inv_s,
    pf,
    psend,
    precv,
    tsh,
    tsend,
    trecv,
    wsend,
    wrecv,
    pwr,
    pbr,
    w2,
    pw2,
    g,
    qkv_s,
    probs_s,
    att_s,
    dqkv_s,
    m_own,
    m_send,
    m_recv,
    b_own,
    b_send,
    b_recv,
    xsend,
    xrecv,
    bxs,
    bxr,
    zown,
    zsend,
    zrecv,
    rs_send,
    rs_recv,
    fin,
    fsend,
    frecv,
    fhs,
    fhr0,
    fhr1,
    outf,
    lsem,
    ssem,
    rsem,
):
    tp = lax.axis_index("tp")
    lon = lax.axis_index("lon")
    core = lax.rem(tp, 2)
    chip = lax.div(tp, 2)
    xh = lax.div(lon, ZL)
    z = lax.rem(lon, ZL)
    sib_tp = chip * 2 + 1 - core
    up = lax.rem(lon + 1, 16)
    down = lax.rem(lon + 15, 16)
    sib = {"tp": sib_tp}
    down_same = {"lon": down}
    up_same = {"lon": up}
    up_cross = {"lon": up, "tp": sib_tp}
    down_cross = {"lon": down, "tp": sib_tp}
    across = {"lon": (1 - xh) * ZL + z}
    chips = [None] + [{"tp": lax.rem(chip + k, CHIPS) * 2 + core} for k in range(1, CHIPS)]
    zs = [None] + [{"lon": xh * ZL + lax.rem(z + k, ZL)} for k in range(1, ZL)]

    barrier = pltpu.get_barrier_semaphore()
    peers = [sib] + chips[1:] + [down_same, up_same, up_cross, down_cross, across] + zs[1:]
    for peer in peers:
        pl.semaphore_signal(barrier, inc=1, device_id=peer, device_id_type=MESH)

    loads = [
        pltpu.make_async_copy(act.at[:, core], act_v, lsem.at[0]),
        pltpu.make_async_copy(og, og_v, lsem.at[1]),
        pltpu.make_async_copy(qw, qw_v, lsem.at[2]),
        pltpu.make_async_copy(pw, pw_v, lsem.at[3]),
        pltpu.make_async_copy(pb, pb_v, lsem.at[4]),
    ]
    for load in loads:
        load.start()

    count = [0]

    def remote(src, dst, peer):
        i = count[0]
        count[0] += 1
        return pltpu.make_async_remote_copy(
            src_ref=src,
            dst_ref=dst,
            send_sem=ssem.at[i],
            recv_sem=rsem.at[i],
            device_id=peer,
            device_id_type=MESH,
        )

    started = []

    def go(copy):
        copy.start()
        started.append(copy)
        return copy

    low = lax.broadcasted_iota(jnp.int32, (1, 128), 1) < HD

    loads[1].wait()
    for l in range(LON):
        both = jnp.concatenate([og_v[l, 0].astype(F32), og_v[l, 1].astype(F32)], axis=1)
        pf[CELLS * l : CELLS * (l + 1), :] = both
    psend[...] = pf[...].astype(BF)

    loads[0].wait()
    for l in range(LON):
        piece = act_v[l].astype(F32)
        if l < 6:
            hs[CELLS * l : CELLS * (l + 1), :] = piece
        else:
            xs[CELLS * (l - 6) : CELLS * (l - 5), :] = piece
    hs[HALF:HPAD, :] = jnp.zeros((HPAD - HALF, D), F32)
    hsend[...] = hs[...].astype(BF)

    loads[2].wait()
    for i in range(4):
        r = pl.ds(256 * i, 256)
        wsend[r, :] = jnp.concatenate(
            [qw_v[0, r].astype(F32), qw_v[1, r].astype(F32)], axis=1
        ).astype(BF)
    for i in range(2):
        a = pl.ds(256 * i, 256)
        b = pl.ds(512 + 256 * i, 256)
        wsend[pl.ds(1024 + 256 * i, 256), :] = jnp.concatenate(
            [qw_v[2, a].astype(F32), qw_v[2, b].astype(F32)], axis=1
        ).astype(BF)
    loads[3].wait()
    loads[4].wait()

    def norm(w):
        def body(i, carry):
            r = pl.ds(pl.multiple_of(WT * w + 48 * i, 16), 48)
            x = xs[r, :]
            cen = x - jnp.mean(x, axis=1, keepdims=True)
            inv = lax.rsqrt(jnp.mean(cen * cen, axis=1, keepdims=True) + 1e-05)
            y = cen * inv
            nf[r, :] = y
            xb[r, :] = y.astype(BF)
            inv_s[r, :] = jnp.broadcast_to(inv, (48, 128))
            return carry

        lax.fori_loop(0, 3, body, 0)

    norm(0)

    pl.semaphore_wait(barrier, len(peers))

    p_copy = go(remote(psend, precv, sib))
    h_copy = go(remote(hsend, hrecv, down_same))
    w_copy = go(remote(wsend, wrecv, sib))
    pw_copy = go(remote(pw_v, pwr, sib))
    pb_copy = go(remote(pb_v, pbr, sib))

    p_copy.wait_recv()
    mine = low == (core == 0)
    merged = jnp.where(mine, pf[...], pltpu.roll(precv[...].astype(F32), HD, 1))
    tsend[...] = merged[0:HPAD].astype(BF)
    t_copy = go(remote(tsend, trecv, down_same))
    tsh[0 : NT - HALF, :] = merged[HALF:NT]
    g[0, chip] = merged[HALF : HALF + WT].astype(BF)
    ag = [[], []]
    for k in range(1, CHIPS):
        ag[0].append(go(remote(g.at[0, chip], g.at[0, chip], chips[k])))

    w_copy.wait_recv()
    for i in range(4):
        r = pl.ds(256 * i, 256)
        got = wrecv[r, :].astype(F32)
        w2[r, 0:128] = jnp.where(
            low, jnp.concatenate([qw_v[0, r].astype(F32)] * 2, axis=1), pltpu.roll(got, HD, 1)
        ).astype(BF)
        w2[r, 128:256] = jnp.where(
            low, jnp.concatenate([qw_v[1, r].astype(F32)] * 2, axis=1), got
        ).astype(BF)
        got = wrecv[pl.ds(1024 + 256 * (i % 2), 256), :].astype(F32)
        if i < 2:
            got = pltpu.roll(got, HD, 1)
        w2[r, 256:384] = jnp.where(
            low, jnp.concatenate([qw_v[2, r].astype(F32)] * 2, axis=1), got
        ).astype(BF)
    wsum = jnp.sum(w2[...].astype(F32), axis=0, keepdims=True)
    pw_copy.wait_recv()
    pw2[0:HD, :] = pw_v[...]
    pw2[HD:128, :] = pwr[...]
    pb_copy.wait_recv()

    def forward(w):
        r = pl.ds(WT * w, WT)
        qkv = nn(xb[r, :], w2[...]).astype(BF)
        qkv_s[r, :] = qkv
        q2, k2, v2 = qkv[:, 0:128], qkv[:, 128:256], qkv[:, 256:384]
        att = []
        for h in range(2):
            keep = low if h == 0 else jnp.logical_not(low)
            s = nt(jnp.where(keep, q2, jnp.zeros_like(q2)), k2) * SCALE
            s = s + (pb_v[0] if h == 0 else pbr[0])
            e = jnp.exp(s - jnp.max(s, axis=1, keepdims=True))
            p = e * (1.0 / jnp.sum(e, axis=1, keepdims=True))
            probs_s[w, h] = p
            att.append(nn(p.astype(BF), v2))
        att_s[r, :] = jnp.where(low, att[0], att[1]).astype(BF)

    forward(0)

    t_copy.wait_recv()
    tsh[NT - HALF : NT, :] = trecv[...].astype(F32)[0:HALF]
    g[1, chip] = tsh[WT:NT, :].astype(BF)
    for k in range(1, CHIPS):
        ag[1].append(go(remote(g.at[1, chip], g.at[1, chip], chips[k])))

    h_copy.wait_recv()
    xs[NT - HALF : NT, :] = hrecv[...].astype(F32)[0:HALF]
    norm(1)
    forward(1)

    def backward(w):
        r = pl.ds(WT * w, WT)
        grads = jnp.concatenate([g[w, m] for m in range(CHIPS)], axis=1)
        ga = nt(grads, pw2[...]).astype(BF)
        q2, k2, v2 = qkv_s[r, 0:128], qkv_s[r, 128:256], qkv_s[r, 256:384]
        dq, dk, dv = [], [], []
        for h in range(2):
            keep = low if h == 0 else jnp.logical_not(low)
            p = probs_s[w, h]
            gp = nt(jnp.where(keep, ga, jnp.zeros_like(ga)), v2)
            ds = p * (gp - jnp.sum(gp * p, axis=1, keepdims=True))
            if w == 0:
                b_own[h] = ds
            else:
                b_own[h] = b_own[h] + ds
            dl = ds.astype(BF)
            dv.append(tn(p.astype(BF), ga))
            dq.append(nn(dl, k2) * SCALE)
            dk.append(tn(dl, q2) * SCALE)
        dqkv_s[r, 0:128] = jnp.where(low, dq[0], dq[1]).astype(BF)
        dqkv_s[r, 128:256] = jnp.where(low, dk[0], dk[1]).astype(BF)
        dqkv_s[r, 256:384] = jnp.where(low, dv[0], dv[1]).astype(BF)

    rs = [[], []]

    def input_grad(w):
        r = pl.ds(WT * w, WT)
        dq = dqkv_s[r, :]
        wide = dq.astype(F32)
        inv = inv_s[r, 0:1]
        first = jnp.sum(wide * wsum, axis=1, keepdims=True) * (1.0 / D)
        second = jnp.sum(wide * qkv_s[r, :].astype(F32), axis=1, keepdims=True) * (1.0 / D)
        for m in range(CHIPS):
            part = nt(dq, w2[128 * m : 128 * (m + 1), :])
            part = inv * (part - first - nf[r, 128 * m : 128 * (m + 1)] * second)
            rs_send[w, m] = part.astype(BF)
        for k in range(1, CHIPS):
            to = lax.rem(chip + k, CHIPS)
            rs[w].append(go(remote(rs_send.at[w, to], rs_recv.at[w, k - 1], chips[k])))

    for copy in ag[0]:
        copy.wait_recv()
    backward(0)
    input_grad(0)

    for copy in ag[1]:
        copy.wait_recv()
    backward(1)

    b_send[:, 0:WT] = b_own[1].astype(BF)
    b_copy = go(remote(b_send, b_recv, sib))
    grads = [jnp.concatenate([g[w, m] for w in range(2)], axis=0) for m in range(CHIPS)]
    for m in range(CHIPS):
        x = xb[:, 128 * m : 128 * (m + 1)]
        for c in range(4):
            if c < 3:
                part = tn(dqkv_s[:, 128 * c : 128 * (c + 1)], x)
            else:
                part = tn(att_s[...], grads[m])
            m_own[m, HD * c : HD * (c + 1), :] = part[0:HD]
            m_send[m, HD * c : HD * (c + 1), :] = part[HD:128].astype(BF)
    far = (1 - xh) * 4
    near = xh * 4
    m_copies = [
        go(remote(m_send.at[pl.ds(far, 4)], m_recv.at[pl.ds(far, 4)], sib)),
        go(remote(m_send.at[pl.ds(near, 4)], m_recv.at[pl.ds(near, 4)], sib)),
    ]

    input_grad(1)

    m_copies[0].wait_recv()
    for j in range(4):
        xsend[j] = (m_own[far + j] + m_recv[far + j].astype(F32)).astype(BF)
    x_copy = go(remote(xsend, xrecv, across))
    b_copy.wait_recv()
    b_own[0] = b_own[0] + b_recv[:, 0:WT].astype(F32)
    half = b_own[0, pl.ds(pl.multiple_of((1 - xh) * HALF, 8), HALF), :]
    bxs[:, 0:WT] = jnp.concatenate([half, jnp.zeros((HPAD - HALF, WT), F32)], axis=0).astype(BF)
    bx_copy = go(remote(bxs, bxr, across))

    def finish(w):
        for copy in rs[w]:
            copy.wait_recv()
        total = tsh[WT * w : WT * (w + 1), :] + rs_send[w, chip].astype(F32)
        for k in range(CHIPS - 1):
            total = total + rs_recv[w, k].astype(F32)
        fin[WT * w : WT * (w + 1), :] = total
        fsend[WT * w : WT * (w + 1), :] = total.astype(BF)

    finish(0)
    f_copies = [go(remote(fsend.at[0:WT], frecv.at[0:WT], sib))]

    m_copies[1].wait_recv()
    x_copy.wait_recv()
    for j in range(4):
        total = m_own[near + j] + m_recv[near + j].astype(F32) + xrecv[j].astype(F32)
        top, bottom = total[0:128], total[128:256]
        even = jnp.where(low, top, pltpu.roll(bottom, HD, 1))
        odd = jnp.where(low, pltpu.roll(top, HD, 1), bottom)
        zown[2 * j, 0:128, :] = even
        zown[2 * j + 1, 0:128, :] = odd
    bx_copy.wait_recv()
    half = b_own[0, pl.ds(pl.multiple_of(xh * HALF, 8), HALF), :] + bxr[...].astype(F32)[0:HALF, 0:WT]
    b_own[1, 0:HALF, :] = half
    for i in range(ZL):
        rows = b_own[1, 9 * i : 9 * (i + 1), :]
        zown[i, 128:137, :] = rows[:, 0:128]
        zown[i, 144:153, 0:16] = rows[:, 128:144]
    zsend[...] = zown[...].astype(BF)
    z_copies = []
    for k in range(1, ZL):
        to = lax.rem(z + k, ZL)
        z_copies.append(go(remote(zsend.at[to], zrecv.at[k - 1], zs[k])))

    finish(1)
    f_copies.append(go(remote(fsend.at[WT : WT + HPAD], frecv.at[WT : WT + HPAD], sib)))
    fhs[...] = jnp.concatenate(
        [fin[NT - HALF : NT, :], jnp.zeros((HPAD - HALF, 128), F32)], axis=0
    ).astype(BF)
    f_copies.append(go(remote(fhs, fhr0, up_same)))
    f_copies.append(go(remote(fhs, fhr1, up_cross)))

    for copy in z_copies:
        copy.wait_recv()
    total = zown[z]
    for k in range(ZL - 1):
        total = total + zrecv[k].astype(F32)
    main = total[0:128]
    out_proj[...] = pltpu.roll(main, HD, 1)[HD:128, 0:HD]
    flip = main.T
    out_qkv[0] = flip[0:HD, 0:HD]
    out_qkv[1] = pltpu.roll(flip, HD, 1)[0:HD, 0:HD]
    out_qkv[2] = flip[HD:128, 0:HD]
    out_bias[0, :, 0:128] = total[128:137]
    out_bias[0, :, 128:144] = total[144:153, 0:16]

    for copy in f_copies:
        copy.wait_recv()

    def chosen(x):
        return jnp.where(core == 0, x, pltpu.roll(x, HD, 1))

    outf[0, 0:HALF, :] = chosen(fhr0[...].astype(F32))[0:HALF]
    outf[0, HALF:NT, :] = chosen(fin[0 : NT - HALF, :])
    outf[1, 0:HALF, :] = chosen(fhr1[...].astype(F32))[0:HALF]
    outf[1, HALF:NT, :] = chosen(frecv[...].astype(F32))[0 : NT - HALF]
    for i in range(2):
        r = core if i == 0 else 1 - core
        for l in range(LON):
            out_in[l, r] = outf[i, CELLS * l : CELLS * (l + 1), 0:HD].astype(BF)

    for copy in started:
        copy.wait_send()


def per_device(activations, qkv_weight, proj_weight, pos_bias, out_grad):
    v = pltpu.VMEM
    scratch = [
        v((LON, CELLS, D), BF),
        v((LON, ROWS, CELLS, HD), BF),
        v((3, D, HD), BF),
        v((HD, D), BF),
        v((1, WT, WT), F32),
        v((NT, D), F32),
        v((HPAD, D), F32),
        v((HPAD, D), BF),
        v((HPAD, D), BF),
        v((NT, D), F32),
        v((NT, D), BF),
        v((NT, 128), F32),
        v((NT, 128), F32),
        v((NT, 128), BF),
        v((NT, 128), BF),
        v((NT, 128), F32),
        v((HPAD, 128), BF),
        v((HPAD, 128), BF),
        v((1536, 128), BF),
        v((1536, 128), BF),
        v((HD, D), BF),
        v((1, WT, WT), F32),
        v((D, 384), BF),
        v((128, D), BF),
        v((2, CHIPS, WT, 128), BF),
        v((NT, 384), BF),
        v((2, 2, WT, WT), F32),
        v((NT, 128), BF),
        v((NT, 384), BF),
        v((CHIPS, 256, 128), F32),
        v((CHIPS, 256, 128), BF),
        v((CHIPS, 256, 128), BF),
        v((2, WT, WT), F32),
        v((WT, 256), BF),
        v((WT, 256), BF),
        v((4, 256, 128), BF),
        v((4, 256, 128), BF),
        v((HPAD, 256), BF),
        v((HPAD, 256), BF),
        v((ZL, 160, 128), F32),
        v((ZL, 160, 128), BF),
        v((ZL - 1, 160, 128), BF),
        v((2, CHIPS, WT, 128), BF),
        v((2, CHIPS - 1, WT, 128), BF),
        v((NT, 128), F32),
        v((NT, 128), BF),
        v((WT + HPAD, 128), BF),
        v((HPAD, 128), BF),
        v((HPAD, 128), BF),
        v((HPAD, 128), BF),
        v((2, NT, 128), F32),
        pltpu.SemaphoreType.DMA((5,)),
        pltpu.SemaphoreType.DMA((56,)),
        pltpu.SemaphoreType.DMA((56,)),
    ]
    hbm = pl.BlockSpec(memory_space=pl.ANY)
    vmem = pl.BlockSpec(memory_space=pltpu.VMEM)
    return pl.pallas_call(
        kernel,
        out_shape=(
            jax.ShapeDtypeStruct((LON, ROWS, CELLS, HD), BF),
            jax.ShapeDtypeStruct((3, HD, HD), F32),
            jax.ShapeDtypeStruct((HD, HD), F32),
            jax.ShapeDtypeStruct((1, 9, WT), F32),
        ),
        in_specs=[hbm] * 5,
        out_specs=(vmem,) * 4,
        scratch_shapes=scratch,
        compiler_params=pltpu.CompilerParams(
            collective_id=0, has_side_effects=True, vmem_limit_bytes=48 << 20
        ),
    )(activations, qkv_weight, proj_weight, pos_bias, out_grad)


def solution(mesh):
    placed = (
        P("lon", None, None, None),
        P(None, None, "tp"),
        P("tp", None),
        P("tp", None, None),
        P("lon", None, None, "tp"),
    )
    return jax.shard_map(
        per_device,
        mesh=mesh,
        in_specs=placed,
        out_specs=(
            P("lon", None, None, "tp"),
            P(None, "lon", "tp"),
            P("tp", "lon"),
            P("tp", "lon", None),
        ),
        check_vma=False,
    )
```

```python
import jax
import jax.numpy as jnp
from jax import lax
from jax.experimental import pallas as pl
from jax.experimental.pallas import tpu as pltpu
from jax.sharding import PartitionSpec as P

BF = jnp.bfloat16
F32 = jnp.float32
MESH = pl.DeviceIdType.MESH

LON = 24
ROWS = 2
CELLS = 12
D = 1024
HD = 64
WT = 144
NT = 288
HALF = 72
HPAD = 80
CHIPS = 8
ZL = 8
SCALE = 0.125


def nt(a, b):
    return lax.dot_general(a, b, (((1,), (1,)), ((), ())), preferred_element_type=F32)


def tn(a, b):
    return lax.dot_general(a, b, (((0,), (0,)), ((), ())), preferred_element_type=F32)


def nn(a, b):
    return jnp.dot(a, b, preferred_element_type=F32)


def kernel(
    act,
    qw,
    pw,
    pb,
    og,
    out,
    act_v,
    og_v,
    xs,
    hs,
    hsend,
    hrecv,
    nf,
    xb,
    inv_s,
    pf,
    psend,
    precv,
    tsh,
    tsend,
    trecv,
    w2,
    pw2,
    pb2,
    g,
    qkv_s,
    probs_s,
    att_s,
    dqkv_s,
    ma_own,
    ma_send,
    ma_recv,
    mb_own,
    mb_send,
    mb_recv,
    b_own,
    b_send,
    b_recv,
    xa_send,
    xa_recv,
    bx_send,
    bx_recv,
    za_own,
    za_send,
    za_recv,
    zb_own,
    zb_send,
    zb_recv,
    xb_send,
    xb_recv,
    rs_send,
    rs_recv,
    fin,
    fsend,
    frecv,
    fhs,
    fhr0,
    fhr1,
    lsem,
    ssem,
    rsem,
):
    tp = lax.axis_index("tp")
    lon = lax.axis_index("lon")
    core = lax.rem(tp, 2)
    chip = lax.div(tp, 2)
    xh = lax.div(lon, ZL)
    z = lax.rem(lon, ZL)
    sib_tp = chip * 2 + 1 - core
    up = lax.rem(lon + 1, 16)
    down = lax.rem(lon + 15, 16)
    sib = {"tp": sib_tp}
    down_same = {"lon": down}
    up_same = {"lon": up}
    up_cross = {"lon": up, "tp": sib_tp}
    down_cross = {"lon": down, "tp": sib_tp}
    across = {"lon": (1 - xh) * ZL + z}
    chips = [None] + [{"tp": lax.rem(chip + k, CHIPS) * 2 + core} for k in range(1, CHIPS)]
    zs = [None] + [{"lon": xh * ZL + lax.rem(z + k, ZL)} for k in range(1, ZL)]

    barrier = pltpu.get_barrier_semaphore()
    peers = [sib] + chips[1:] + [down_same, up_same, up_cross, down_cross, across] + zs[1:]
    for peer in peers:
        pl.semaphore_signal(barrier, inc=1, device_id=peer, device_id_type=MESH)

    loads = [
        pltpu.make_async_copy(og, og_v, lsem.at[0]),
        pltpu.make_async_copy(qw, w2.at[:, 0], lsem.at[1]),
        pltpu.make_async_copy(pw, pw2.at[0], lsem.at[2]),
        pltpu.make_async_copy(pb.at[0], pb2.at[0], lsem.at[3]),
        pltpu.make_async_copy(act, act_v, lsem.at[4]),
    ]
    for load in loads:
        load.start()

    count = [0]

    def remote(src, dst, peer):
        i = count[0]
        count[0] += 1
        return pltpu.make_async_remote_copy(
            src_ref=src,
            dst_ref=dst,
            send_sem=ssem.at[i],
            recv_sem=rsem.at[i],
            device_id=peer,
            device_id_type=MESH,
        )

    started = []

    def go(copy):
        copy.start()
        started.append(copy)
        return copy

    low = lax.broadcasted_iota(jnp.int32, (1, 128), 1) < HD

    loads[0].wait()
    for l in range(LON):
        both = og_v[l].astype(F32)
        pf[CELLS * l : CELLS * (l + 1), :] = jnp.concatenate([both[:, 0], both[:, 1]], axis=1)
    psend[...] = pf[...].astype(BF)

    pl.semaphore_wait(barrier, len(peers))

    p_copy = go(remote(psend, precv, sib))
    for load in loads[1:4]:
        load.wait()
    w_copy = go(remote(w2.at[:, 0], w2.at[:, 1], sib))
    pw_copy = go(remote(pw2.at[0], pw2.at[1], sib))
    pb_copy = go(remote(pb2.at[0], pb2.at[1], sib))

    loads[4].wait()

    def row_of(l):
        both = act_v[l].astype(F32)
        return jnp.where(core == 0, both[:, 0], both[:, 1])

    for l in range(6):
        hs[CELLS * l : CELLS * (l + 1), :] = row_of(l)
    hs[HALF:HPAD, :] = jnp.zeros((HPAD - HALF, D), F32)
    hsend[...] = hs[...].astype(BF)
    h_copy = go(remote(hsend, hrecv, down_same))

    p_copy.wait_recv()
    mine = low == (core == 0)
    merged = jnp.where(mine, pf[...], pltpu.roll(precv[...].astype(F32), HD, 1))
    tsend[...] = merged[0:HPAD].astype(BF)
    t_copy = go(remote(tsend, trecv, down_same))
    tsh[0 : NT - HALF, :] = merged[HALF:NT]
    g[0, chip] = merged[HALF : HALF + WT].astype(BF)
    ag = [[], []]
    for k in range(1, CHIPS):
        ag[0].append(go(remote(g.at[0, chip], g.at[0, chip], chips[k])))

    for l in range(6, LON):
        xs[CELLS * (l - 6) : CELLS * (l - 5), :] = row_of(l)

    def norm(w):
        def body(i, carry):
            r = pl.ds(pl.multiple_of(WT * w + 48 * i, 16), 48)
            x = xs[r, :]
            cen = x - jnp.mean(x, axis=1, keepdims=True)
            inv = lax.rsqrt(jnp.mean(cen * cen, axis=1, keepdims=True) + 1e-05)
            y = cen * inv
            nf[r, :] = y
            xb[r, :] = y.astype(BF)
            inv_s[r, :] = jnp.broadcast_to(inv, (48, 128))
            return carry

        lax.fori_loop(0, 3, body, 0)

    t_copy.wait_recv()
    tsh[NT - HALF : NT, :] = trecv[...].astype(F32)[0:HALF]
    g[1, chip] = tsh[WT:NT, :].astype(BF)
    for k in range(1, CHIPS):
        ag[1].append(go(remote(g.at[1, chip], g.at[1, chip], chips[k])))

    norm(0)
    w_copy.wait_recv()
    pw_copy.wait_recv()
    pb_copy.wait_recv()

    def weights():
        return w2[...].reshape(6 * HD, D)

    wsum = nt(jnp.ones((8, D), BF), weights())[0:1]

    def forward(w):
        r = pl.ds(WT * w, WT)
        qkv = nt(xb[r, :], weights()).astype(BF)
        qkv_s[r, :] = qkv
        q2, k2, v2 = qkv[:, 0:128], qkv[:, 128:256], qkv[:, 256:384]
        att = []
        for h in range(2):
            keep = low if h == 0 else jnp.logical_not(low)
            s = nt(jnp.where(keep, q2, jnp.zeros_like(q2)), k2) * SCALE + pb2[h]
            e = jnp.exp(s - jnp.max(s, axis=1, keepdims=True))
            p = e * (1.0 / jnp.sum(e, axis=1, keepdims=True))
            probs_s[w, h] = p
            att.append(nn(p.astype(BF), v2))
        att_s[r, :] = jnp.where(low, att[0], att[1]).astype(BF)

    forward(0)

    h_copy.wait_recv()
    xs[NT - HALF : NT, :] = hrecv[...].astype(F32)[0:HALF]
    norm(1)
    forward(1)

    def backward(w):
        r = pl.ds(WT * w, WT)
        grads = jnp.concatenate([g[w, m] for m in range(CHIPS)], axis=1)
        ga = nt(grads, pw2[...].reshape(2 * HD, D)).astype(BF)
        q2, k2, v2 = qkv_s[r, 0:128], qkv_s[r, 128:256], qkv_s[r, 256:384]
        dq, dk, dv = [], [], []
        for h in range(2):
            keep = low if h == 0 else jnp.logical_not(low)
            p = probs_s[w, h]
            gp = nt(jnp.where(keep, ga, jnp.zeros_like(ga)), v2)
            ds = p * (gp - jnp.sum(gp * p, axis=1, keepdims=True))
            if w == 0:
                b_own[h] = ds
            else:
                b_own[h] = b_own[h] + ds
            dl = ds.astype(BF)
            dv.append(tn(p.astype(BF), ga))
            dq.append(nn(dl, k2) * SCALE)
            dk.append(tn(dl, q2) * SCALE)
        dqkv_s[r, 0:128] = jnp.where(low, dq[0], dq[1]).astype(BF)
        dqkv_s[r, 128:256] = jnp.where(low, dk[0], dk[1]).astype(BF)
        dqkv_s[r, 256:384] = jnp.where(low, dv[0], dv[1]).astype(BF)

    rs = [[], []]

    def input_grad(w):
        r = pl.ds(WT * w, WT)
        dq = dqkv_s[r, :]
        wide = dq.astype(F32)
        inv = inv_s[r, 0:1]
        first = jnp.sum(wide * wsum, axis=1, keepdims=True) * (1.0 / D)
        second = jnp.sum(wide * qkv_s[r, :].astype(F32), axis=1, keepdims=True) * (1.0 / D)
        for m in range(CHIPS):
            lanes = slice(128 * m, 128 * (m + 1))
            part = nn(dq, w2[:, :, :, lanes].reshape(6 * HD, 128))
            part = inv * (part - first - nf[r, lanes] * second)
            rs_send[w, m] = part.astype(BF)
        for k in range(1, CHIPS):
            to = lax.rem(chip + k, CHIPS)
            rs[w].append(go(remote(rs_send.at[w, to], rs_recv.at[w, k - 1], chips[k])))

    for copy in ag[0]:
        copy.wait_recv()
    backward(0)
    input_grad(0)

    for copy in ag[1]:
        copy.wait_recv()
    backward(1)

    def weight_grad(parts, own, send):
        for m in range(CHIPS):
            for i, c in enumerate(parts):
                if c < 3:
                    left, right = dqkv_s[:, 128 * c : 128 * (c + 1)], xb[:, 128 * m : 128 * (m + 1)]
                else:
                    left = att_s[...]
                    right = jnp.concatenate([g[0, m], g[1, m]], axis=0)
                part = tn(left, right)
                own[m, HD * i : HD * (i + 1), :] = part[0:HD]
                send[m, HD * i : HD * (i + 1), :] = part[HD:128].astype(BF)

    weight_grad((1, 3), mb_own, mb_send)
    mb_copy = go(remote(mb_send, mb_recv, sib))
    b_send[:, 0:WT] = b_own[1].astype(BF)
    b_copy = go(remote(b_send, b_recv, sib))
    weight_grad((0, 2), ma_own, ma_send)
    far = (1 - xh) * 4
    near = xh * 4
    ma_copies = [
        go(remote(ma_send.at[pl.ds(i, 4)], ma_recv.at[pl.ds(i, 4)], sib)) for i in (far, near)
    ]

    def packed(total):
        top, bottom = total[0:HD], total[HD:128]
        return (
            jnp.where(low, top, pltpu.roll(bottom, HD, 1)),
            jnp.where(low, pltpu.roll(top, HD, 1), bottom),
        )

    mb_copy.wait_recv()
    for m in range(CHIPS):
        even, odd = packed(mb_own[m] + mb_recv[m].astype(F32))
        to = (2 * m) % ZL
        zb_own[to, m // 4] = even
        zb_own[to + 1, m // 4] = odd
        zb_send[to, m // 4] = even.astype(BF)
        zb_send[to + 1, m // 4] = odd.astype(BF)
    zb_copies = []
    for k in range(1, ZL):
        to = lax.rem(z + k, ZL)
        zb_copies.append(go(remote(zb_send.at[to], zb_recv.at[k - 1], zs[k])))

    ma_copies[0].wait_recv()
    for j in range(4):
        xa_send[j] = (ma_own[far + j] + ma_recv[far + j].astype(F32)).astype(BF)
    xa_copy = go(remote(xa_send, xa_recv, across))
    b_copy.wait_recv()
    b_own[0] = b_own[0] + b_recv[:, 0:WT].astype(F32)
    half = b_own[0, pl.ds(pl.multiple_of((1 - xh) * HALF, 8), HALF), :]
    bx_send[:, 0:WT] = jnp.concatenate([half, jnp.zeros((HPAD - HALF, WT), F32)], axis=0).astype(BF)
    bx_copy = go(remote(bx_send, bx_recv, across))

    input_grad(1)

    def finish(w):
        for copy in rs[w]:
            copy.wait_recv()
        total = tsh[WT * w : WT * (w + 1), :] + rs_send[w, chip].astype(F32)
        for k in range(CHIPS - 1):
            total = total + rs_recv[w, k].astype(F32)
        fin[WT * w : WT * (w + 1), :] = total
        fsend[WT * w : WT * (w + 1), :] = total.astype(BF)

    finish(0)
    f_copies = [go(remote(fsend.at[0:WT], frecv.at[0:WT], sib))]
    finish(1)
    fhs[...] = jnp.concatenate(
        [fin[NT - HALF : NT, :], jnp.zeros((HPAD - HALF, 128), F32)], axis=0
    ).astype(BF)
    f_copies.append(go(remote(fhs, fhr0, up_same)))
    f_copies.append(go(remote(fhs, fhr1, up_cross)))
    f_copies.append(go(remote(fsend.at[WT : WT + HPAD], frecv.at[WT : WT + HPAD], sib)))

    ma_copies[1].wait_recv()
    xa_copy.wait_recv()
    for j in range(4):
        even, odd = packed(ma_own[near + j] + ma_recv[near + j].astype(F32) + xa_recv[j].astype(F32))
        za_own[2 * j, 0:HD, :] = even
        za_own[2 * j + 1, 0:HD, :] = odd
    bx_copy.wait_recv()
    half = b_own[0, pl.ds(pl.multiple_of(xh * HALF, 8), HALF), :]
    b_own[1, 0:HALF, :] = half + bx_recv[...].astype(F32)[0:HALF, 0:WT]
    for i in range(ZL):
        rows = b_own[1, 9 * i : 9 * (i + 1), :]
        za_own[i, HD : HD + 9, :] = rows[:, 0:128]
        za_own[i, HD + 16 : HD + 25, 0:16] = rows[:, 128:144]
    za_send[...] = za_own[...].astype(BF)
    za_copies = []
    for k in range(1, ZL):
        to = lax.rem(z + k, ZL)
        za_copies.append(go(remote(za_send.at[to], za_recv.at[k - 1], zs[k])))

    for copy in zb_copies:
        copy.wait_recv()

    def over_z(part):
        total = zb_own[z, part]
        for k in range(ZL - 1):
            total = total + zb_recv[k, part].astype(F32)
        return total

    xb_send[...] = over_z(1 - xh).astype(BF)
    xb_copy = go(remote(xb_send, xb_recv, across))
    second_half = over_z(xh)

    for copy in f_copies:
        copy.wait_recv()

    def chosen(x):
        return jnp.where(core == 0, x, pltpu.roll(x, HD, 1))

    here = jnp.concatenate([chosen(fhr0[...].astype(F32))[0:HALF], chosen(fin[0 : NT - HALF, :])], axis=0)
    there = jnp.concatenate(
        [chosen(fhr1[...].astype(F32))[0:HALF], chosen(frecv[...].astype(F32))[0 : NT - HALF]], axis=0
    )
    out[0:NT, :] = jnp.where(
        low, jnp.where(core == 0, here, there), pltpu.roll(jnp.where(core == 0, there, here), HD, 1)
    )

    xb_copy.wait_recv()
    out[NT : NT + HD, :] = second_half + xb_recv[...].astype(F32)

    for copy in za_copies:
        copy.wait_recv()
    total = za_own[z]
    for k in range(ZL - 1):
        total = total + za_recv[k].astype(F32)
    out[NT + HD : NT + HD + 96, :] = total

    for copy in started:
        copy.wait_send()


def unpack(parts, out_in, out_qkv, out_proj, out_bias):
    for l in range(LON):
        x = parts[CELLS * l : CELLS * (l + 1), :]
        out_in[l] = jnp.stack([x[:, 0:HD], x[:, HD:128]], axis=1).astype(BF)
    key_proj = parts[NT : NT + HD, :]
    query_value = parts[NT + HD : NT + 2 * HD, :].T
    out_qkv[0] = query_value[0:HD]
    out_qkv[1] = key_proj.T[0:HD]
    out_qkv[2] = query_value[HD:128]
    out_proj[...] = pltpu.roll(key_proj, HD, 1)[:, 0:HD]
    at = NT + 2 * HD
    out_bias[:, 0, 0:128] = parts[at : at + 9, :]
    out_bias[:, 0, 128:144] = parts[at + 16 : at + 25, 0:16]


def per_device(activations, qkv_weight, proj_weight, pos_bias, out_grad):
    v = pltpu.VMEM
    scratch = [
        v((LON, CELLS, ROWS, D), BF),
        v((LON, CELLS, ROWS, HD), BF),
        v((NT, D), F32),
        v((HPAD, D), F32),
        v((HPAD, D), BF),
        v((HPAD, D), BF),
        v((NT, D), F32),
        v((NT, D), BF),
        v((NT, 128), F32),
        v((NT, 128), F32),
        v((NT, 128), BF),
        v((NT, 128), BF),
        v((NT, 128), F32),
        v((HPAD, 128), BF),
        v((HPAD, 128), BF),
        v((3, 2, HD, D), BF),
        v((2, HD, D), BF),
        v((2, WT, WT), F32),
        v((2, CHIPS, WT, 128), BF),
        v((NT, 384), BF),
        v((2, 2, WT, WT), F32),
        v((NT, 128), BF),
        v((NT, 384), BF),
        v((CHIPS, 128, 128), F32),
        v((CHIPS, 128, 128), BF),
        v((CHIPS, 128, 128), BF),
        v((CHIPS, 128, 128), F32),
        v((CHIPS, 128, 128), BF),
        v((CHIPS, 128, 128), BF),
        v((2, WT, WT), F32),
        v((WT, 256), BF),
        v((WT, 256), BF),
        v((4, 128, 128), BF),
        v((4, 128, 128), BF),
        v((HPAD, 256), BF),
        v((HPAD, 256), BF),
        v((ZL, 96, 128), F32),
        v((ZL, 96, 128), BF),
        v((ZL - 1, 96, 128), BF),
        v((ZL, 2, HD, 128), F32),
        v((ZL, 2, HD, 128), BF),
        v((ZL - 1, 2, HD, 128), BF),
        v((HD, 128), BF),
        v((HD, 128), BF),
        v((2, CHIPS, WT, 128), BF),
        v((2, CHIPS - 1, WT, 128), BF),
        v((NT, 128), F32),
        v((NT, 128), BF),
        v((WT + HPAD, 128), BF),
        v((HPAD, 128), BF),
        v((HPAD, 128), BF),
        v((HPAD, 128), BF),
        pltpu.SemaphoreType.DMA((5,)),
        pltpu.SemaphoreType.DMA((64,)),
        pltpu.SemaphoreType.DMA((64,)),
    ]
    hbm = pl.BlockSpec(memory_space=pl.ANY)
    vmem = pl.BlockSpec(memory_space=pltpu.VMEM)
    shapes = (
        jax.ShapeDtypeStruct((LON, CELLS, ROWS, HD), BF),
        jax.ShapeDtypeStruct((3, HD, HD), F32),
        jax.ShapeDtypeStruct((HD, HD), F32),
        jax.ShapeDtypeStruct((9, 1, WT), F32),
    )
    parts = pl.pallas_call(
        kernel,
        out_shape=jax.ShapeDtypeStruct((NT + HD + 96, 128), F32),
        in_specs=[hbm] * 5,
        out_specs=vmem,
        scratch_shapes=scratch,
        compiler_params=pltpu.CompilerParams(
            collective_id=0, has_side_effects=True, vmem_limit_bytes=60 << 20
        ),
    )(
        activations.transpose(0, 2, 1, 3),
        qkv_weight.transpose(0, 2, 1),
        proj_weight,
        pos_bias,
        out_grad.transpose(0, 2, 1, 3),
    )
    in_grad, qkv_grad, proj_grad, bias_grad = pl.pallas_call(
        unpack,
        out_shape=shapes,
        in_specs=[vmem],
        out_specs=(vmem,) * 4,
        compiler_params=pltpu.CompilerParams(vmem_limit_bytes=60 << 20),
    )(parts)
    return in_grad.transpose(0, 2, 1, 3), qkv_grad, proj_grad, bias_grad.transpose(1, 0, 2)


def solution(mesh):
    placed = (
        P("lon", None, None, None),
        P(None, None, "tp"),
        P("tp", None),
        P("tp", None, None),
        P("lon", None, None, "tp"),
    )
    return jax.shard_map(
        per_device,
        mesh=mesh,
        in_specs=placed,
        out_specs=(
            P("lon", None, None, "tp"),
            P(None, "lon", "tp"),
            P("tp", "lon"),
            P("tp", "lon", None),
        ),
        check_vma=False,
    )
```

```python
import jax
import jax.numpy as jnp
from jax import lax
from jax.experimental import pallas as pl
from jax.experimental.pallas import tpu as pltpu
from jax.sharding import PartitionSpec as P

BF = jnp.bfloat16
F32 = jnp.float32
MESH = pl.DeviceIdType.MESH

LON = 24
ROWS = 2
CELLS = 12
D = 1024
HD = 64
WT = 144
NT = 288
HALF = 72
HPAD = 80
CHIPS = 8
ZL = 8
SCALE = 0.125


def nt(a, b):
    return lax.dot_general(a, b, (((1,), (1,)), ((), ())), preferred_element_type=F32)


def tn(a, b):
    return lax.dot_general(a, b, (((0,), (0,)), ((), ())), preferred_element_type=F32)


def nn(a, b):
    return jnp.dot(a, b, preferred_element_type=F32)


def kernel(
    act,
    qw,
    pw,
    pb,
    og,
    out,
    act_v,
    og_v,
    xs,
    hs,
    hsend,
    hrecv,
    nf,
    xb,
    inv_s,
    pf,
    psend,
    precv,
    tsh,
    tsend,
    trecv,
    w2,
    pw2,
    pb2,
    g,
    qkv_s,
    probs_s,
    att_s,
    dqkv_s,
    ma_own,
    ma_send,
    ma_recv,
    mk_own,
    mk_send,
    mk_recv,
    mp_own,
    mp_send,
    mp_recv,
    b_own,
    b_send,
    b_recv,
    xa_send,
    xa_recv,
    bx_send,
    bx_recv,
    za_own,
    za_send,
    za_recv,
    zk_own,
    zk_send,
    zk_recv,
    zp_own,
    zp_send,
    zp_recv,
    xb_send,
    xb_recv,
    rs_send,
    rs_recv,
    rx_send,
    rx_recv,
    fin,
    fsend,
    frecv,
    fhs,
    fhr0,
    fhr1,
    lsem,
    ssem,
    rsem,
):
    tp = lax.axis_index("tp")
    lon = lax.axis_index("lon")
    core = lax.rem(tp, 2)
    chip = lax.div(tp, 2)
    xh = lax.div(lon, ZL)
    z = lax.rem(lon, ZL)
    sib_tp = chip * 2 + 1 - core
    up = lax.rem(lon + 1, 16)
    down = lax.rem(lon + 15, 16)
    sib = {"tp": sib_tp}
    down_same = {"lon": down}
    up_same = {"lon": up}
    up_cross = {"lon": up, "tp": sib_tp}
    down_cross = {"lon": down, "tp": sib_tp}
    across = {"lon": (1 - xh) * ZL + z}
    chips = [None] + [{"tp": lax.rem(chip + k, CHIPS) * 2 + core} for k in range(1, CHIPS)]
    row, side = lax.div(chip, 2), lax.rem(chip, 2)
    ys = [None] + [{"tp": (lax.rem(row + k, 4) * 2 + side) * 2 + core} for k in range(1, 4)]
    beside = {"tp": (row * 2 + 1 - side) * 2 + core}
    zs = [None] + [{"lon": xh * ZL + lax.rem(z + k, ZL)} for k in range(1, ZL)]

    barrier = pltpu.get_barrier_semaphore()
    peers = [sib] + chips[1:] + [down_same, up_same, up_cross, down_cross, across] + zs[1:]
    for peer in peers:
        pl.semaphore_signal(barrier, inc=1, device_id=peer, device_id_type=MESH)

    loads = [
        pltpu.make_async_copy(og, og_v, lsem.at[0]),
        pltpu.make_async_copy(qw, w2.at[:, 0], lsem.at[1]),
        pltpu.make_async_copy(pw, pw2.at[0], lsem.at[2]),
        pltpu.make_async_copy(pb.at[0], pb2.at[0], lsem.at[3]),
        pltpu.make_async_copy(act, act_v, lsem.at[4]),
    ]
    for load in loads:
        load.start()

    count = [0]

    def remote(src, dst, peer):
        i = count[0]
        count[0] += 1
        return pltpu.make_async_remote_copy(
            src_ref=src,
            dst_ref=dst,
            send_sem=ssem.at[i],
            recv_sem=rsem.at[i],
            device_id=peer,
            device_id_type=MESH,
        )

    started = []

    def go(copy):
        copy.start()
        started.append(copy)
        return copy

    low = lax.broadcasted_iota(jnp.int32, (1, 128), 1) < HD

    loads[0].wait()
    for l in range(LON):
        both = og_v[l].astype(F32)
        pf[CELLS * l : CELLS * (l + 1), :] = jnp.concatenate([both[:, 0], both[:, 1]], axis=1)
    psend[...] = pf[...].astype(BF)

    pl.semaphore_wait(barrier, len(peers))

    p_copy = go(remote(psend, precv, sib))
    for load in loads[1:4]:
        load.wait()
    w_copy = go(remote(w2.at[:, 0], w2.at[:, 1], sib))
    pw_copy = go(remote(pw2.at[0], pw2.at[1], sib))
    pb_copy = go(remote(pb2.at[0], pb2.at[1], sib))

    loads[4].wait()

    def row_of(l):
        both = act_v[l].astype(F32)
        return jnp.where(core == 0, both[:, 0], both[:, 1])

    for l in range(6):
        hs[CELLS * l : CELLS * (l + 1), :] = row_of(l)
    hs[HALF:HPAD, :] = jnp.zeros((HPAD - HALF, D), F32)
    hsend[...] = hs[...].astype(BF)
    h_copy = go(remote(hsend, hrecv, down_same))

    p_copy.wait_recv()
    mine = low == (core == 0)
    merged = jnp.where(mine, pf[...], pltpu.roll(precv[...].astype(F32), HD, 1))
    tsend[...] = merged[0:HPAD].astype(BF)
    t_copy = go(remote(tsend, trecv, down_same))
    tsh[0 : NT - HALF, :] = merged[HALF:NT]
    g[0, chip] = merged[HALF : HALF + WT].astype(BF)
    ag = [[], []]
    for k in range(1, CHIPS):
        ag[0].append(go(remote(g.at[0, chip], g.at[0, chip], chips[k])))

    for l in range(6, LON):
        xs[CELLS * (l - 6) : CELLS * (l - 5), :] = row_of(l)

    def norm(w):
        def body(i, carry):
            r = pl.ds(pl.multiple_of(WT * w + 48 * i, 16), 48)
            x = xs[r, :]
            cen = x - jnp.mean(x, axis=1, keepdims=True)
            inv = lax.rsqrt(jnp.mean(cen * cen, axis=1, keepdims=True) + 1e-05)
            y = cen * inv
            nf[r, :] = y
            xb[r, :] = y.astype(BF)
            inv_s[r, :] = jnp.broadcast_to(inv, (48, 128))
            return carry

        lax.fori_loop(0, 3, body, 0)

    t_copy.wait_recv()
    tsh[NT - HALF : NT, :] = trecv[...].astype(F32)[0:HALF]
    g[1, chip] = tsh[WT:NT, :].astype(BF)
    for k in range(1, CHIPS):
        ag[1].append(go(remote(g.at[1, chip], g.at[1, chip], chips[k])))

    norm(0)
    w_copy.wait_recv()
    pw_copy.wait_recv()
    pb_copy.wait_recv()

    def weights():
        return w2[...].reshape(6 * HD, D)

    wsum = nt(jnp.ones((8, D), BF), weights())[0:1]

    def forward(w):
        r = pl.ds(WT * w, WT)
        qkv = nt(xb[r, :], weights()).astype(BF)
        qkv_s[r, :] = qkv
        q2, k2, v2 = qkv[:, 0:128], qkv[:, 128:256], qkv[:, 256:384]
        att = []
        for h in range(2):
            keep = low if h == 0 else jnp.logical_not(low)
            s = nt(jnp.where(keep, q2, jnp.zeros_like(q2)), k2) * SCALE + pb2[h]
            e = jnp.exp(s - jnp.max(s, axis=1, keepdims=True))
            p = e * (1.0 / jnp.sum(e, axis=1, keepdims=True))
            probs_s[w, h] = p
            att.append(nn(p.astype(BF), v2))
        att_s[r, :] = jnp.where(low, att[0], att[1]).astype(BF)

    forward(0)

    h_copy.wait_recv()
    xs[NT - HALF : NT, :] = hrecv[...].astype(F32)[0:HALF]
    norm(1)
    forward(1)

    def backward(w):
        r = pl.ds(WT * w, WT)
        grads = jnp.concatenate([g[w, m] for m in range(CHIPS)], axis=1)
        ga = nt(grads, pw2[...].reshape(2 * HD, D)).astype(BF)
        q2, k2, v2 = qkv_s[r, 0:128], qkv_s[r, 128:256], qkv_s[r, 256:384]
        dq, dk, dv = [], [], []
        for h in range(2):
            keep = low if h == 0 else jnp.logical_not(low)
            p = probs_s[w, h]
            gp = nt(jnp.where(keep, ga, jnp.zeros_like(ga)), v2)
            ds = p * (gp - jnp.sum(gp * p, axis=1, keepdims=True))
            if w == 0:
                b_own[h] = ds
            else:
                b_own[h] = b_own[h] + ds
            dl = ds.astype(BF)
            dv.append(tn(p.astype(BF), ga))
            dq.append(nn(dl, k2) * SCALE)
            dk.append(tn(dl, q2) * SCALE)
        dqkv_s[r, 0:128] = jnp.where(low, dq[0], dq[1]).astype(BF)
        dqkv_s[r, 128:256] = jnp.where(low, dk[0], dk[1]).astype(BF)
        dqkv_s[r, 256:384] = jnp.where(low, dv[0], dv[1]).astype(BF)

    early, late, halo, rest = (0, 0, 80), (0, 80, 64), (1, 64, 80), (1, 0, 64)
    rs = {}

    def send_out(part):
        w, a, n = part
        rows = pl.ds(a, n)
        rs[part] = []
        for k in range(1, 4):
            to = lax.rem(row + k, 4)
            rs[part].append(
                go(remote(rs_send.at[w, to, :, rows], rs_recv.at[w, k - 1, :, rows], ys[k]))
            )

    def input_grad(w):
        r = pl.ds(WT * w, WT)
        dq = dqkv_s[r, :]
        wide = dq.astype(F32)
        inv = inv_s[r, 0:1]
        first = jnp.sum(wide * wsum, axis=1, keepdims=True) * (1.0 / D)
        second = jnp.sum(wide * qkv_s[r, :].astype(F32), axis=1, keepdims=True) * (1.0 / D)
        for m in range(CHIPS):
            lanes = slice(128 * m, 128 * (m + 1))
            part = nn(dq, w2[:, :, :, lanes].reshape(6 * HD, 128))
            part = inv * (part - first - nf[r, lanes] * second)
            rs_send[w, m // 2, m % 2] = part.astype(BF)

    for copy in ag[0]:
        copy.wait_recv()
    backward(0)
    input_grad(0)

    for copy in ag[1]:
        copy.wait_recv()
    send_out(late)

    def weight_grad(parts, own, send):
        for m in range(CHIPS):
            for i, c in enumerate(parts):
                if c < 3:
                    left, right = dqkv_s[:, 128 * c : 128 * (c + 1)], xb[:, 128 * m : 128 * (m + 1)]
                else:
                    left = att_s[...]
                    right = jnp.concatenate([g[0, m], g[1, m]], axis=0)
                part = tn(left, right)
                own[m, HD * i : HD * (i + 1), :] = part[0:HD]
                send[m, HD * i : HD * (i + 1), :] = part[HD:128].astype(BF)

    weight_grad((3,), mp_own, mp_send)
    mp_copy = go(remote(mp_send, mp_recv, sib))
    backward(1)

    input_grad(1)
    send_out(halo)
    b_send[:, 0:WT] = b_own[1].astype(BF)
    b_copy = go(remote(b_send, b_recv, sib))
    weight_grad((0, 2), ma_own, ma_send)
    far = (1 - xh) * 4
    near = xh * 4
    ma_copies = [
        go(remote(ma_send.at[pl.ds(i, 4)], ma_recv.at[pl.ds(i, 4)], sib)) for i in (far, near)
    ]

    def packed(total):
        top, bottom = total[0:HD], total[HD:128]
        return (
            jnp.where(low, top, pltpu.roll(bottom, HD, 1)),
            jnp.where(low, pltpu.roll(top, HD, 1), bottom),
        )

    def start_z(copy, own, recv, z_own, z_send, z_recv):
        copy.wait_recv()
        for m in range(4):
            first = own[m] + recv[m].astype(F32)
            second = own[m + 4] + recv[m + 4].astype(F32)
            even = jnp.where(low, first, pltpu.roll(second, HD, 1))
            odd = jnp.where(low, pltpu.roll(first, HD, 1), second)
            z_own[2 * m] = even
            z_own[2 * m + 1] = odd
            z_send[2 * m] = even.astype(BF)
            z_send[2 * m + 1] = odd.astype(BF)
        out = []
        for k in range(1, ZL):
            to = lax.rem(z + k, ZL)
            out.append(go(remote(z_send.at[to], z_recv.at[k - 1], zs[k])))
        return out

    zp_copies = start_z(mp_copy, mp_own, mp_recv, zp_own, zp_send, zp_recv)
    weight_grad((1,), mk_own, mk_send)
    mk_copy = go(remote(mk_send, mk_recv, sib))
    send_out(early)
    send_out(rest)

    ma_copies[0].wait_recv()
    for j in range(4):
        xa_send[j] = (ma_own[far + j] + ma_recv[far + j].astype(F32)).astype(BF)
    xa_copy = go(remote(xa_send, xa_recv, across))
    zk_copies = start_z(mk_copy, mk_own, mk_recv, zk_own, zk_send, zk_recv)
    b_copy.wait_recv()
    b_own[0] = b_own[0] + b_recv[:, 0:WT].astype(F32)
    half = b_own[0, pl.ds(pl.multiple_of((1 - xh) * HALF, 8), HALF), :]
    bx_send[0:HPAD, :] = jnp.concatenate(
        [half[:, 0:128], jnp.zeros((HPAD - HALF, 128), F32)], axis=0
    ).astype(BF)
    bx_send[HPAD:96, 0:HALF] = half[:, 128:WT].T.astype(BF)
    bx_copy = go(remote(bx_send, bx_recv, across))


    def over_y(part, which):
        w, a, n = part
        rows = slice(a, a + n)
        total = rs_send[w, row, which, rows].astype(F32)
        for k in range(3):
            total = total + rs_recv[w, k, which, rows].astype(F32)
        return total

    def pass_over(part):
        w, a, n = part
        rows = pl.ds(a, n)
        for copy in rs[part]:
            copy.wait_recv()
        rx_send[w, rows] = over_y(part, 1 - side).astype(BF)
        return go(remote(rx_send.at[w, rows], rx_recv.at[w, rows], beside))

    def finish(part, copy):
        w, a, n = part
        r = slice(WT * w + a, WT * w + a + n)
        total = tsh[r, :] + over_y(part, side)
        copy.wait_recv()
        total = total + rx_recv[w, a : a + n].astype(F32)
        fin[r, :] = total
        fsend[r, :] = total.astype(BF)

    rx_late = pass_over(late)
    rx_halo = pass_over(halo)
    finish(late, rx_late)
    finish(halo, rx_halo)
    moved = jnp.concatenate([fin[NT - HALF : NT, :], jnp.zeros((HPAD - HALF, 128), F32)], axis=0)
    turned = pltpu.roll(moved, HD, 1)
    firsts = jnp.where(low, moved[0:40], turned[40:80])
    seconds = jnp.where(low, turned[0:40], moved[40:80])
    mine_half = jnp.where(core == 0, firsts, seconds)
    other_half = jnp.where(core == 0, seconds, firsts)
    blank = jnp.zeros((8, 128), F32)
    fhs[0] = jnp.concatenate([mine_half, blank], axis=0).astype(BF)
    fhs[1] = jnp.concatenate([other_half, blank], axis=0).astype(BF)
    f_copies = [go(remote(fhs.at[0], fhr0, up_same)), go(remote(fhs.at[1], fhr1, up_cross))]

    ma_copies[1].wait_recv()
    xa_copy.wait_recv()
    for j in range(4):
        even, odd = packed(ma_own[near + j] + ma_recv[near + j].astype(F32) + xa_recv[j].astype(F32))
        za_own[2 * j, 0:HD, :] = even
        za_own[2 * j + 1, 0:HD, :] = odd
    bx_copy.wait_recv()
    half = b_own[0, pl.ds(pl.multiple_of(xh * HALF, 8), HALF), :]
    b_own[1, 0:HALF, 0:128] = half[:, 0:128] + bx_recv[...].astype(F32)[0:HALF]
    b_own[1, 0:HALF, 128:WT] = half[:, 128:WT] + bx_recv[HPAD:96, 0:HALF].astype(F32).T
    for i in range(ZL):
        rows = b_own[1, 9 * i : 9 * (i + 1), :]
        za_own[i, HD : HD + 9, :] = rows[:, 0:128]
        za_own[i, HD + 9 : HD + 16, 0:16] = rows[0:7, 128:144]
        za_own[i, HD + 9 : HD + 11, 16:32] = rows[7:9, 128:144]
    za_send[...] = za_own[...].astype(BF)
    za_copies = []
    for k in range(1, ZL):
        to = lax.rem(z + k, ZL)
        za_copies.append(go(remote(za_send.at[to], za_recv.at[k - 1], zs[k])))

    rx_early = pass_over(early)
    rx_rest = pass_over(rest)
    finish(early, rx_early)
    f_copies.append(go(remote(fsend.at[0:WT], frecv.at[0:WT], sib)))
    finish(rest, rx_rest)
    f_copies.append(go(remote(fsend.at[WT : WT + HPAD], frecv.at[WT : WT + HPAD], sib)))

    def over_z(copies, z_own, z_recv):
        for copy in copies:
            copy.wait_recv()
        total = z_own[z]
        for k in range(ZL - 1):
            total = total + z_recv[k].astype(F32)
        return total, pltpu.roll(total, HD, 1)

    proj_sum, proj_turned = over_z(zp_copies, zp_own, zp_recv)
    key_sum, key_turned = over_z(zk_copies, zk_own, zk_recv)
    ahead = jnp.where(low, key_sum, proj_turned)
    behind = jnp.where(low, key_turned, proj_sum)
    xb_send[...] = jnp.where(xh == 0, behind, ahead).astype(BF)
    xb_copy = go(remote(xb_send, xb_recv, across))
    second_half = jnp.where(xh == 0, ahead, behind)

    for copy in f_copies:
        copy.wait_recv()

    def chosen(x):
        return jnp.where(core == 0, x, pltpu.roll(x, HD, 1))

    def opened(half):
        half = half[...].astype(F32)[0:40]
        return jnp.concatenate([half, pltpu.roll(half, HD, 1)], axis=0)[0:HALF]

    here = jnp.concatenate([opened(fhr0), chosen(fin[0 : NT - HALF, :])], axis=0)
    there = jnp.concatenate([opened(fhr1), chosen(frecv[...].astype(F32))[0 : NT - HALF]], axis=0)
    out[0:NT, :] = jnp.where(
        low, jnp.where(core == 0, here, there), pltpu.roll(jnp.where(core == 0, there, here), HD, 1)
    )

    xb_copy.wait_recv()
    out[NT : NT + HD, :] = second_half + xb_recv[...].astype(F32)

    for copy in za_copies:
        copy.wait_recv()
    total = za_own[z]
    for k in range(ZL - 1):
        total = total + za_recv[k].astype(F32)
    out[NT + HD : NT + HD + 80, :] = total

    for copy in started:
        copy.wait_send()


def unpack(parts, out_in, out_qkv, out_proj, out_bias):
    for l in range(LON):
        x = parts[CELLS * l : CELLS * (l + 1), :]
        out_in[l] = jnp.stack([x[:, 0:HD], x[:, HD:128]], axis=1).astype(BF)
    key_proj = parts[NT : NT + HD, :]
    query_value = parts[NT + HD : NT + 2 * HD, :].T
    out_qkv[0] = query_value[0:HD]
    out_qkv[1] = key_proj.T[0:HD]
    out_qkv[2] = query_value[HD:128]
    out_proj[...] = pltpu.roll(key_proj, HD, 1)[:, 0:HD]
    at = NT + 2 * HD
    out_bias[:, 0, 0:128] = parts[at : at + 9, :]
    out_bias[0:7, 0, 128:144] = parts[at + 9 : at + 16, 0:16]
    out_bias[7:9, 0, 128:144] = parts[at + 9 : at + 11, 16:32]


def per_device(activations, qkv_weight, proj_weight, pos_bias, out_grad):
    v = pltpu.VMEM
    scratch = [
        v((LON, CELLS, ROWS, D), BF),
        v((LON, CELLS, ROWS, HD), BF),
        v((NT, D), F32),
        v((HPAD, D), F32),
        v((HPAD, D), BF),
        v((HPAD, D), BF),
        v((NT, D), F32),
        v((NT, D), BF),
        v((NT, 128), F32),
        v((NT, 128), F32),
        v((NT, 128), BF),
        v((NT, 128), BF),
        v((NT, 128), F32),
        v((HPAD, 128), BF),
        v((HPAD, 128), BF),
        v((3, 2, HD, D), BF),
        v((2, HD, D), BF),
        v((2, WT, WT), F32),
        v((2, CHIPS, WT, 128), BF),
        v((NT, 384), BF),
        v((2, 2, WT, WT), F32),
        v((NT, 128), BF),
        v((NT, 384), BF),
        v((CHIPS, 128, 128), F32),
        v((CHIPS, 128, 128), BF),
        v((CHIPS, 128, 128), BF),
        v((CHIPS, HD, 128), F32),
        v((CHIPS, HD, 128), BF),
        v((CHIPS, HD, 128), BF),
        v((CHIPS, HD, 128), F32),
        v((CHIPS, HD, 128), BF),
        v((CHIPS, HD, 128), BF),
        v((2, WT, WT), F32),
        v((WT, 256), BF),
        v((WT, 256), BF),
        v((4, 128, 128), BF),
        v((4, 128, 128), BF),
        v((96, 128), BF),
        v((96, 128), BF),
        v((ZL, 80, 128), F32),
        v((ZL, 80, 128), BF),
        v((ZL - 1, 80, 128), BF),
        v((ZL, HD, 128), F32),
        v((ZL, HD, 128), BF),
        v((ZL - 1, HD, 128), BF),
        v((ZL, HD, 128), F32),
        v((ZL, HD, 128), BF),
        v((ZL - 1, HD, 128), BF),
        v((HD, 128), BF),
        v((HD, 128), BF),
        v((2, 4, 2, WT, 128), BF),
        v((2, 3, 2, WT, 128), BF),
        v((2, WT, 128), BF),
        v((2, WT, 128), BF),
        v((NT, 128), F32),
        v((NT, 128), BF),
        v((WT + HPAD, 128), BF),
        v((2, 48, 128), BF),
        v((48, 128), BF),
        v((48, 128), BF),
        pltpu.SemaphoreType.DMA((5,)),
        pltpu.SemaphoreType.DMA((72,)),
        pltpu.SemaphoreType.DMA((72,)),
    ]
    hbm = pl.BlockSpec(memory_space=pl.ANY)
    vmem = pl.BlockSpec(memory_space=pltpu.VMEM)
    shapes = (
        jax.ShapeDtypeStruct((LON, CELLS, ROWS, HD), BF),
        jax.ShapeDtypeStruct((3, HD, HD), F32),
        jax.ShapeDtypeStruct((HD, HD), F32),
        jax.ShapeDtypeStruct((9, 1, WT), F32),
    )
    parts = pl.pallas_call(
        kernel,
        out_shape=jax.ShapeDtypeStruct((NT + HD + 80, 128), F32),
        in_specs=[hbm] * 5,
        out_specs=vmem,
        scratch_shapes=scratch,
        compiler_params=pltpu.CompilerParams(
            collective_id=0, has_side_effects=True, vmem_limit_bytes=60 << 20
        ),
    )(
        activations.transpose(0, 2, 1, 3),
        qkv_weight.transpose(0, 2, 1),
        proj_weight,
        pos_bias,
        out_grad.transpose(0, 2, 1, 3),
    )
    in_grad, qkv_grad, proj_grad, bias_grad = pl.pallas_call(
        unpack,
        out_shape=shapes,
        in_specs=[vmem],
        out_specs=(vmem,) * 4,
        compiler_params=pltpu.CompilerParams(vmem_limit_bytes=60 << 20),
    )(parts)
    return in_grad.transpose(0, 2, 1, 3), qkv_grad, proj_grad, bias_grad.transpose(1, 0, 2)


def solution(mesh):
    placed = (
        P("lon", None, None, None),
        P(None, None, "tp"),
        P("tp", None),
        P("tp", None, None),
        P("lon", None, None, "tp"),
    )
    return jax.shard_map(
        per_device,
        mesh=mesh,
        in_specs=placed,
        out_specs=(
            P("lon", None, None, "tp"),
            P(None, "lon", "tp"),
            P("tp", "lon"),
            P("tp", "lon", None),
        ),
        check_vma=False,
    )
```

```python
import jax
import jax.numpy as jnp
from jax import lax
from jax.experimental import pallas as pl
from jax.experimental.pallas import tpu as pltpu
from jax.sharding import PartitionSpec as P

BF = jnp.bfloat16
F32 = jnp.float32
MESH = pl.DeviceIdType.MESH

LON = 24
ROWS = 2
CELLS = 12
D = 1024
HD = 64
WT = 144
NT = 288
HALF = 72
HPAD = 80
CHIPS = 8
ZL = 8
SCALE = 0.125


def nt(a, b):
    return lax.dot_general(a, b, (((1,), (1,)), ((), ())), preferred_element_type=F32)


def tn(a, b):
    return lax.dot_general(a, b, (((0,), (0,)), ((), ())), preferred_element_type=F32)


def nn(a, b):
    return jnp.dot(a, b, preferred_element_type=F32)


def kernel(
    act,
    qw,
    pw,
    pb,
    og,
    out,
    act_v,
    og_v,
    xs,
    hs,
    hsend,
    hrecv,
    nf,
    xb,
    inv_s,
    pf,
    psend,
    precv,
    tsh,
    town,
    tsend,
    trecv,
    w2,
    pw2,
    pb2,
    g,
    qkv_s,
    probs_s,
    att_s,
    dqkv_s,
    ma_own,
    ma_send,
    ma_recv,
    mk_own,
    mk_send,
    mk_recv,
    mp_own,
    mp_send,
    mp_recv,
    b_own,
    b_send,
    b_recv,
    xa_send,
    xa_recv,
    bx_send,
    bx_recv,
    za_own,
    za_send,
    za_recv,
    zk_own,
    zk_send,
    zk_recv,
    zp_own,
    zp_send,
    zp_recv,
    xb_send,
    xb_recv,
    rs_send,
    rs_recv,
    rx_send,
    rx_recv,
    fin,
    fsend,
    frecv,
    hr_recv,
    up_send,
    up_recv,
    fh_send,
    fh_recv,
    lsem,
    ssem,
    rsem,
):
    tp = lax.axis_index("tp")
    lon = lax.axis_index("lon")
    core = lax.rem(tp, 2)
    chip = lax.div(tp, 2)
    xh = lax.div(lon, ZL)
    z = lax.rem(lon, ZL)
    sib_tp = chip * 2 + 1 - core
    up = lax.rem(lon + 1, 16)
    down = lax.rem(lon + 15, 16)
    sib = {"tp": sib_tp}
    down_same = {"lon": down}
    up_same = {"lon": up}
    across = {"lon": (1 - xh) * ZL + z}
    chips = [None] + [{"tp": lax.rem(chip + k, CHIPS) * 2 + core} for k in range(1, CHIPS)]
    row, side = lax.div(chip, 2), lax.rem(chip, 2)
    ys = [None] + [{"tp": (lax.rem(row + k, 4) * 2 + side) * 2 + core} for k in range(1, 4)]
    beside_tp = (row * 2 + 1 - side) * 2 + core
    beside = {"tp": beside_tp}
    up_beside = {"lon": up, "tp": beside_tp}
    down_beside = {"lon": down, "tp": beside_tp}
    zs = [None] + [{"lon": xh * ZL + lax.rem(z + k, ZL)} for k in range(1, ZL)]

    barrier = pltpu.get_barrier_semaphore()
    peers = [sib] + chips[1:] + [down_same, up_same, up_beside, down_beside, across] + zs[1:]
    for peer in peers:
        pl.semaphore_signal(barrier, inc=1, device_id=peer, device_id_type=MESH)

    loads = [
        pltpu.make_async_copy(og, og_v, lsem.at[0]),
        pltpu.make_async_copy(qw, w2.at[:, 0], lsem.at[1]),
        pltpu.make_async_copy(pw, pw2.at[0], lsem.at[2]),
        pltpu.make_async_copy(pb.at[0], pb2.at[0], lsem.at[3]),
        pltpu.make_async_copy(act, act_v, lsem.at[4]),
    ]
    for load in loads:
        load.start()

    count = [0]

    def remote(src, dst, peer):
        i = count[0]
        count[0] += 1
        return pltpu.make_async_remote_copy(
            src_ref=src,
            dst_ref=dst,
            send_sem=ssem.at[i],
            recv_sem=rsem.at[i],
            device_id=peer,
            device_id_type=MESH,
        )

    started = []

    def go(copy):
        copy.start()
        started.append(copy)
        return copy

    low = lax.broadcasted_iota(jnp.int32, (1, 128), 1) < HD

    loads[0].wait()
    for l in range(LON):
        both = og_v[l].astype(F32)
        pf[CELLS * l : CELLS * (l + 1), :] = jnp.concatenate([both[:, 0], both[:, 1]], axis=1)
    psend[...] = pf[...].astype(BF)

    pl.semaphore_wait(barrier, len(peers))

    p_copy = go(remote(psend, precv, sib))
    for load in loads[1:4]:
        load.wait()
    w_copy = go(remote(w2.at[:, 0], w2.at[:, 1], sib))
    pw_copy = go(remote(pw2.at[0], pw2.at[1], sib))
    pb_copy = go(remote(pb2.at[0], pb2.at[1], sib))

    loads[4].wait()

    def row_of(l):
        both = act_v[l].astype(F32)
        return jnp.where(core == 0, both[:, 0], both[:, 1])

    for l in range(6):
        hs[CELLS * l : CELLS * (l + 1), :] = row_of(l)
    hs[HALF:HPAD, :] = jnp.zeros((HPAD - HALF, D), F32)
    hsend[...] = hs[...].astype(BF)
    h_copy = go(remote(hsend, hrecv, down_same))

    p_copy.wait_recv()
    mine = low == (core == 0)
    merged = jnp.where(mine, pf[...], pltpu.roll(precv[...].astype(F32), HD, 1))
    town[...] = merged[0:HPAD]
    tsend[...] = merged[0:HPAD].astype(BF)
    t_copy = go(remote(tsend, trecv, down_same))
    tsh[0 : NT - HALF, :] = merged[HALF:NT]
    g[0, chip] = merged[HALF : HALF + WT].astype(BF)
    ag = [[], []]
    for k in range(1, CHIPS):
        ag[0].append(go(remote(g.at[0, chip], g.at[0, chip], chips[k])))

    for l in range(6, LON):
        xs[CELLS * (l - 6) : CELLS * (l - 5), :] = row_of(l)

    def norm(w):
        def body(i, carry):
            r = pl.ds(pl.multiple_of(WT * w + 48 * i, 16), 48)
            x = xs[r, :]
            cen = x - jnp.mean(x, axis=1, keepdims=True)
            inv = lax.rsqrt(jnp.mean(cen * cen, axis=1, keepdims=True) + 1e-05)
            y = cen * inv
            nf[r, :] = y
            xb[r, :] = y.astype(BF)
            inv_s[r, :] = jnp.broadcast_to(inv, (48, 128))
            return carry

        lax.fori_loop(0, 3, body, 0)

    t_copy.wait_recv()
    tsh[NT - HALF : NT, :] = trecv[...].astype(F32)[0:HALF]
    g[1, chip] = tsh[WT:NT, :].astype(BF)
    for k in range(1, CHIPS):
        ag[1].append(go(remote(g.at[1, chip], g.at[1, chip], chips[k])))

    norm(0)
    w_copy.wait_recv()
    pw_copy.wait_recv()
    pb_copy.wait_recv()

    def weights():
        return w2[...].reshape(6 * HD, D)

    wsum = nt(jnp.ones((8, D), BF), weights())[0:1]

    def forward(w):
        r = pl.ds(WT * w, WT)
        qkv = nt(xb[r, :], weights()).astype(BF)
        qkv_s[r, :] = qkv
        q2, k2, v2 = qkv[:, 0:128], qkv[:, 128:256], qkv[:, 256:384]
        att = []
        for h in range(2):
            keep = low if h == 0 else jnp.logical_not(low)
            s = nt(jnp.where(keep, q2, jnp.zeros_like(q2)), k2) * SCALE + pb2[h]
            e = jnp.exp(s - jnp.max(s, axis=1, keepdims=True))
            p = e * (1.0 / jnp.sum(e, axis=1, keepdims=True))
            probs_s[w, h] = p
            att.append(nn(p.astype(BF), v2))
        att_s[r, :] = jnp.where(low, att[0], att[1]).astype(BF)

    forward(0)

    h_copy.wait_recv()
    xs[NT - HALF : NT, :] = hrecv[...].astype(F32)[0:HALF]
    norm(1)
    forward(1)

    def backward(w):
        r = pl.ds(WT * w, WT)
        grads = jnp.concatenate([g[w, m] for m in range(CHIPS)], axis=1)
        ga = nt(grads, pw2[...].reshape(2 * HD, D)).astype(BF)
        q2, k2, v2 = qkv_s[r, 0:128], qkv_s[r, 128:256], qkv_s[r, 256:384]
        dq, dk, dv = [], [], []
        for h in range(2):
            keep = low if h == 0 else jnp.logical_not(low)
            p = probs_s[w, h]
            gp = nt(jnp.where(keep, ga, jnp.zeros_like(ga)), v2)
            ds = p * (gp - jnp.sum(gp * p, axis=1, keepdims=True))
            if w == 0:
                b_own[h] = ds
            else:
                b_own[h] = b_own[h] + ds
            dl = ds.astype(BF)
            dv.append(tn(p.astype(BF), ga))
            dq.append(nn(dl, k2) * SCALE)
            dk.append(tn(dl, q2) * SCALE)
        dqkv_s[r, 0:128] = jnp.where(low, dq[0], dq[1]).astype(BF)
        dqkv_s[r, 128:256] = jnp.where(low, dk[0], dk[1]).astype(BF)
        dqkv_s[r, 256:384] = jnp.where(low, dv[0], dv[1]).astype(BF)

    early, late, rest = (0, 0, 80), (0, 80, 64), (1, 0, 80)
    rs = {}
    over = pl.ds(WT - HPAD, HPAD)

    def send_out(part):
        w, a, n = part
        rows = pl.ds(a, n)
        rs[part] = []
        for k in range(1, 4):
            to = lax.rem(row + k, 4)
            rs[part].append(
                go(remote(rs_send.at[w, to, :, rows], rs_recv.at[w, k - 1, :, rows], ys[k]))
            )

    def input_grad(w):
        r = pl.ds(WT * w, WT)
        dq = dqkv_s[r, :]
        wide = dq.astype(F32)
        inv = inv_s[r, 0:1]
        first = jnp.sum(wide * wsum, axis=1, keepdims=True) * (1.0 / D)
        second = jnp.sum(wide * qkv_s[r, :].astype(F32), axis=1, keepdims=True) * (1.0 / D)
        for m in range(CHIPS):
            lanes = slice(128 * m, 128 * (m + 1))
            part = nn(dq, w2[:, :, :, lanes].reshape(6 * HD, 128))
            part = inv * (part - first - nf[r, lanes] * second)
            rs_send[w, m // 2, m % 2] = part.astype(BF)

    for copy in ag[0]:
        copy.wait_recv()
    backward(0)
    input_grad(0)

    for copy in ag[1]:
        copy.wait_recv()
    send_out(late)

    def weight_grad(parts, own, send):
        for m in range(CHIPS):
            for i, c in enumerate(parts):
                if c < 3:
                    left, right = dqkv_s[:, 128 * c : 128 * (c + 1)], xb[:, 128 * m : 128 * (m + 1)]
                else:
                    left = att_s[...]
                    right = jnp.concatenate([g[0, m], g[1, m]], axis=0)
                part = tn(left, right)
                own[m, HD * i : HD * (i + 1), :] = part[0:HD]
                send[m, HD * i : HD * (i + 1), :] = part[HD:128].astype(BF)

    weight_grad((3,), mp_own, mp_send)
    mp_copy = go(remote(mp_send, mp_recv, sib))
    backward(1)

    input_grad(1)
    halo_copies = []
    for k in range(1, 4):
        to = lax.rem(row + k, 4)
        halo_copies.append(go(remote(rs_send.at[1, to, :, over], hr_recv.at[k - 1], ys[k])))
    b_send[:, 0:WT] = b_own[1].astype(BF)
    b_copy = go(remote(b_send, b_recv, sib))
    weight_grad((0, 2), ma_own, ma_send)
    far = (1 - xh) * 4
    near = xh * 4
    ma_copies = [
        go(remote(ma_send.at[pl.ds(i, 4)], ma_recv.at[pl.ds(i, 4)], sib)) for i in (far, near)
    ]

    def packed(total):
        top, bottom = total[0:HD], total[HD:128]
        return (
            jnp.where(low, top, pltpu.roll(bottom, HD, 1)),
            jnp.where(low, pltpu.roll(top, HD, 1), bottom),
        )

    def start_z(copy, own, recv, z_own, z_send, z_recv):
        copy.wait_recv()
        for m in range(4):
            first = own[m] + recv[m].astype(F32)
            second = own[m + 4] + recv[m + 4].astype(F32)
            even = jnp.where(low, first, pltpu.roll(second, HD, 1))
            odd = jnp.where(low, pltpu.roll(first, HD, 1), second)
            z_own[2 * m] = even
            z_own[2 * m + 1] = odd
            z_send[2 * m] = even.astype(BF)
            z_send[2 * m + 1] = odd.astype(BF)
        out = []
        for k in range(1, ZL):
            to = lax.rem(z + k, ZL)
            out.append(go(remote(z_send.at[to], z_recv.at[k - 1], zs[k])))
        return out

    zp_copies = start_z(mp_copy, mp_own, mp_recv, zp_own, zp_send, zp_recv)
    weight_grad((1,), mk_own, mk_send)
    mk_copy = go(remote(mk_send, mk_recv, sib))
    send_out(early)
    send_out(rest)

    ma_copies[0].wait_recv()
    for j in range(4):
        xa_send[j] = (ma_own[far + j] + ma_recv[far + j].astype(F32)).astype(BF)
    xa_copy = go(remote(xa_send, xa_recv, across))
    zk_copies = start_z(mk_copy, mk_own, mk_recv, zk_own, zk_send, zk_recv)
    b_copy.wait_recv()
    b_own[0] = b_own[0] + b_recv[:, 0:WT].astype(F32)
    half = b_own[0, pl.ds(pl.multiple_of((1 - xh) * HALF, 8), HALF), :]
    bx_send[0:HPAD, :] = jnp.concatenate(
        [half[:, 0:128], jnp.zeros((HPAD - HALF, 128), F32)], axis=0
    ).astype(BF)
    bx_send[HPAD:96, 0:HALF] = half[:, 128:WT].T.astype(BF)
    bx_copy = go(remote(bx_send, bx_recv, across))


    def over_y(part, which):
        w, a, n = part
        rows = slice(a, a + n)
        total = rs_send[w, row, which, rows].astype(F32)
        for k in range(3):
            total = total + rs_recv[w, k, which, rows].astype(F32)
        return total

    def pass_over(part):
        w, a, n = part
        rows = pl.ds(a, n)
        for copy in rs[part]:
            copy.wait_recv()
        rx_send[w, rows] = over_y(part, 1 - side).astype(BF)
        return go(remote(rx_send.at[w, rows], rx_recv.at[w, rows], beside))

    def finish(part, copy):
        w, a, n = part
        r = slice(WT * w + a, WT * w + a + n)
        total = tsh[r, :] + over_y(part, side)
        copy.wait_recv()
        total = total + rx_recv[w, a : a + n].astype(F32)
        fin[r, :] = total
        fsend[r, :] = total.astype(BF)

    rx_late = pass_over(late)
    for copy in halo_copies:
        copy.wait_recv()
    for i, (which, peer) in enumerate([(side, up_same), (1 - side, up_beside)]):
        total = rs_send[1, row, which, over].astype(F32)
        for k in range(3):
            total = total + hr_recv[k, which].astype(F32)
        up_send[i] = total.astype(BF)
    up_copies = [
        go(remote(up_send.at[i], up_recv.at[i], peer)) for i, peer in enumerate((up_same, up_beside))
    ]
    finish(late, rx_late)
    f_copies = []

    ma_copies[1].wait_recv()
    xa_copy.wait_recv()
    for j in range(4):
        even, odd = packed(ma_own[near + j] + ma_recv[near + j].astype(F32) + xa_recv[j].astype(F32))
        za_own[2 * j, 0:HD, :] = even
        za_own[2 * j + 1, 0:HD, :] = odd
    bx_copy.wait_recv()
    half = b_own[0, pl.ds(pl.multiple_of(xh * HALF, 8), HALF), :]
    b_own[1, 0:HALF, 0:128] = half[:, 0:128] + bx_recv[...].astype(F32)[0:HALF]
    b_own[1, 0:HALF, 128:WT] = half[:, 128:WT] + bx_recv[HPAD:96, 0:HALF].astype(F32).T
    for i in range(ZL):
        rows = b_own[1, 9 * i : 9 * (i + 1), :]
        za_own[i, HD : HD + 9, :] = rows[:, 0:128]
        za_own[i, HD + 9 : HD + 16, 0:16] = rows[0:7, 128:144]
        za_own[i, HD + 9 : HD + 11, 16:32] = rows[7:9, 128:144]
    za_send[...] = za_own[...].astype(BF)
    za_copies = []
    for k in range(1, ZL):
        to = lax.rem(z + k, ZL)
        za_copies.append(go(remote(za_send.at[to], za_recv.at[k - 1], zs[k])))

    rx_early = pass_over(early)
    rx_rest = pass_over(rest)
    for copy in up_copies:
        copy.wait_recv()
    moved = up_recv[0].astype(F32) + up_recv[1].astype(F32)
    moved = moved[HPAD - HALF : HPAD] + town[0:HALF]
    fh_send[...] = jnp.concatenate([moved, jnp.zeros((HPAD - HALF, 128), F32)], axis=0).astype(BF)
    f_copies.append(go(remote(fh_send, fh_recv, sib)))
    finish(early, rx_early)
    f_copies.append(go(remote(fsend.at[0:WT], frecv.at[0:WT], sib)))
    finish(rest, rx_rest)
    f_copies.append(go(remote(fsend.at[WT : WT + HPAD], frecv.at[WT : WT + HPAD], sib)))

    def over_z(copies, z_own, z_recv):
        for copy in copies:
            copy.wait_recv()
        total = z_own[z]
        for k in range(ZL - 1):
            total = total + z_recv[k].astype(F32)
        return total, pltpu.roll(total, HD, 1)

    proj_sum, proj_turned = over_z(zp_copies, zp_own, zp_recv)
    key_sum, key_turned = over_z(zk_copies, zk_own, zk_recv)
    ahead = jnp.where(low, key_sum, proj_turned)
    behind = jnp.where(low, key_turned, proj_sum)
    xb_send[...] = jnp.where(xh == 0, behind, ahead).astype(BF)
    xb_copy = go(remote(xb_send, xb_recv, across))
    second_half = jnp.where(xh == 0, ahead, behind)

    for copy in f_copies:
        copy.wait_recv()

    def chosen(x):
        return jnp.where(core == 0, x, pltpu.roll(x, HD, 1))

    here = chosen(jnp.concatenate([moved, fin[0 : NT - HALF, :]], axis=0))
    there = jnp.concatenate([fh_recv[...].astype(F32)[0:HALF], frecv[...].astype(F32)[0 : NT - HALF]], axis=0)
    there = chosen(there)
    out[0:NT, :] = jnp.where(
        low, jnp.where(core == 0, here, there), pltpu.roll(jnp.where(core == 0, there, here), HD, 1)
    )

    xb_copy.wait_recv()
    out[NT : NT + HD, :] = second_half + xb_recv[...].astype(F32)

    for copy in za_copies:
        copy.wait_recv()
    total = za_own[z]
    for k in range(ZL - 1):
        total = total + za_recv[k].astype(F32)
    out[NT + HD : NT + HD + 80, :] = total

    for copy in started:
        copy.wait_send()


def unpack(parts, out_in, out_qkv, out_proj, out_bias):
    for l in range(LON):
        x = parts[CELLS * l : CELLS * (l + 1), :]
        out_in[l] = jnp.stack([x[:, 0:HD], x[:, HD:128]], axis=1).astype(BF)
    key_proj = parts[NT : NT + HD, :]
    query_value = parts[NT + HD : NT + 2 * HD, :].T
    out_qkv[0] = query_value[0:HD]
    out_qkv[1] = key_proj.T[0:HD]
    out_qkv[2] = query_value[HD:128]
    out_proj[...] = pltpu.roll(key_proj, HD, 1)[:, 0:HD]
    at = NT + 2 * HD
    out_bias[:, 0, 0:128] = parts[at : at + 9, :]
    out_bias[0:7, 0, 128:144] = parts[at + 9 : at + 16, 0:16]
    out_bias[7:9, 0, 128:144] = parts[at + 9 : at + 11, 16:32]


def per_device(activations, qkv_weight, proj_weight, pos_bias, out_grad):
    v = pltpu.VMEM
    scratch = [
        v((LON, CELLS, ROWS, D), BF),
        v((LON, CELLS, ROWS, HD), BF),
        v((NT, D), F32),
        v((HPAD, D), F32),
        v((HPAD, D), BF),
        v((HPAD, D), BF),
        v((NT, D), F32),
        v((NT, D), BF),
        v((NT, 128), F32),
        v((NT, 128), F32),
        v((NT, 128), BF),
        v((NT, 128), BF),
        v((NT, 128), F32),
        v((HPAD, 128), F32),
        v((HPAD, 128), BF),
        v((HPAD, 128), BF),
        v((3, 2, HD, D), BF),
        v((2, HD, D), BF),
        v((2, WT, WT), F32),
        v((2, CHIPS, WT, 128), BF),
        v((NT, 384), BF),
        v((2, 2, WT, WT), F32),
        v((NT, 128), BF),
        v((NT, 384), BF),
        v((CHIPS, 128, 128), F32),
        v((CHIPS, 128, 128), BF),
        v((CHIPS, 128, 128), BF),
        v((CHIPS, HD, 128), F32),
        v((CHIPS, HD, 128), BF),
        v((CHIPS, HD, 128), BF),
        v((CHIPS, HD, 128), F32),
        v((CHIPS, HD, 128), BF),
        v((CHIPS, HD, 128), BF),
        v((2, WT, WT), F32),
        v((WT, 256), BF),
        v((WT, 256), BF),
        v((4, 128, 128), BF),
        v((4, 128, 128), BF),
        v((96, 128), BF),
        v((96, 128), BF),
        v((ZL, 80, 128), F32),
        v((ZL, 80, 128), BF),
        v((ZL - 1, 80, 128), BF),
        v((ZL, HD, 128), F32),
        v((ZL, HD, 128), BF),
        v((ZL - 1, HD, 128), BF),
        v((ZL, HD, 128), F32),
        v((ZL, HD, 128), BF),
        v((ZL - 1, HD, 128), BF),
        v((HD, 128), BF),
        v((HD, 128), BF),
        v((2, 4, 2, WT, 128), BF),
        v((2, 3, 2, WT, 128), BF),
        v((2, WT, 128), BF),
        v((2, WT, 128), BF),
        v((NT, 128), F32),
        v((NT, 128), BF),
        v((WT + HPAD, 128), BF),
        v((3, 2, HPAD, 128), BF),
        v((2, HPAD, 128), BF),
        v((2, HPAD, 128), BF),
        v((HPAD, 128), BF),
        v((HPAD, 128), BF),
        pltpu.SemaphoreType.DMA((5,)),
        pltpu.SemaphoreType.DMA((72,)),
        pltpu.SemaphoreType.DMA((72,)),
    ]
    hbm = pl.BlockSpec(memory_space=pl.ANY)
    vmem = pl.BlockSpec(memory_space=pltpu.VMEM)
    shapes = (
        jax.ShapeDtypeStruct((LON, CELLS, ROWS, HD), BF),
        jax.ShapeDtypeStruct((3, HD, HD), F32),
        jax.ShapeDtypeStruct((HD, HD), F32),
        jax.ShapeDtypeStruct((9, 1, WT), F32),
    )
    parts = pl.pallas_call(
        kernel,
        out_shape=jax.ShapeDtypeStruct((NT + HD + 80, 128), F32),
        in_specs=[hbm] * 5,
        out_specs=vmem,
        scratch_shapes=scratch,
        compiler_params=pltpu.CompilerParams(
            collective_id=0, has_side_effects=True, vmem_limit_bytes=60 << 20
        ),
    )(
        activations.transpose(0, 2, 1, 3),
        qkv_weight.transpose(0, 2, 1),
        proj_weight,
        pos_bias,
        out_grad.transpose(0, 2, 1, 3),
    )
    in_grad, qkv_grad, proj_grad, bias_grad = pl.pallas_call(
        unpack,
        out_shape=shapes,
        in_specs=[vmem],
        out_specs=(vmem,) * 4,
        compiler_params=pltpu.CompilerParams(vmem_limit_bytes=60 << 20),
    )(parts)
    return in_grad.transpose(0, 2, 1, 3), qkv_grad, proj_grad, bias_grad.transpose(1, 0, 2)


def solution(mesh):
    placed = (
        P("lon", None, None, None),
        P(None, None, "tp"),
        P("tp", None),
        P("tp", None, None),
        P("lon", None, None, "tp"),
    )
    return jax.shard_map(
        per_device,
        mesh=mesh,
        in_specs=placed,
        out_specs=(
            P("lon", None, None, "tp"),
            P(None, "lon", "tp"),
            P("tp", "lon"),
            P("tp", "lon", None),
        ),
        check_vma=False,
    )
```

```python
import jax
import jax.numpy as jnp
from jax import lax
from jax.experimental import pallas as pl
from jax.experimental.pallas import tpu as pltpu
from jax.sharding import PartitionSpec as P

BF = jnp.bfloat16
F32 = jnp.float32
MESH = pl.DeviceIdType.MESH

LON = 24
ROWS = 2
CELLS = 12
D = 1024
HD = 64
WT = 144
NT = 288
HALF = 72
HPAD = 80
CHIPS = 8
ZL = 8
SCALE = 0.125


def nt(a, b):
    return lax.dot_general(a, b, (((1,), (1,)), ((), ())), preferred_element_type=F32)


def tn(a, b):
    return lax.dot_general(a, b, (((0,), (0,)), ((), ())), preferred_element_type=F32)


def nn(a, b):
    return jnp.dot(a, b, preferred_element_type=F32)


def kernel(
    act,
    qw,
    pw,
    pb,
    og,
    out,
    act_v,
    og_v,
    xs,
    hs,
    hsend,
    hrecv,
    nf,
    xb,
    inv_s,
    pf,
    psend,
    precv,
    tsh,
    town,
    tsend,
    trecv,
    w2,
    pw2,
    pb2,
    g,
    qkv_s,
    probs_s,
    att_s,
    dqkv_s,
    ma_own,
    ma_send,
    ma_recv,
    mk_own,
    mk_send,
    mk_recv,
    mp_own,
    mp_send,
    mp_recv,
    b_own,
    b_send,
    b_recv,
    xa_send,
    xa_recv,
    bx_send,
    bx_recv,
    za_own,
    za_send,
    za_recv,
    zk_own,
    zk_send,
    zk_recv,
    zp_own,
    zp_send,
    zp_recv,
    xb_send,
    xb_recv,
    rs_send,
    rs_recv,
    rx_send,
    rx_recv,
    fin,
    fsend,
    frecv,
    hr_recv,
    up_send,
    up_recv,
    fh_send,
    fh_recv,
    lsem,
    ssem,
    rsem,
):
    tp = lax.axis_index("tp")
    lon = lax.axis_index("lon")
    core = lax.rem(tp, 2)
    chip = lax.div(tp, 2)
    xh = lax.div(lon, ZL)
    z = lax.rem(lon, ZL)
    sib_tp = chip * 2 + 1 - core
    up = lax.rem(lon + 1, 16)
    down = lax.rem(lon + 15, 16)
    sib = {"tp": sib_tp}
    down_same = {"lon": down}
    up_same = {"lon": up}
    across = {"lon": (1 - xh) * ZL + z}
    chips = [None] + [{"tp": lax.rem(chip + k, CHIPS) * 2 + core} for k in range(1, CHIPS)]
    row, side = lax.div(chip, 2), lax.rem(chip, 2)
    ys = [None] + [{"tp": (lax.rem(row + k, 4) * 2 + side) * 2 + core} for k in range(1, 4)]
    beside_tp = (row * 2 + 1 - side) * 2 + core
    beside = {"tp": beside_tp}
    up_beside = {"lon": up, "tp": beside_tp}
    down_beside = {"lon": down, "tp": beside_tp}
    zs = [None] + [{"lon": xh * ZL + lax.rem(z + k, ZL)} for k in range(1, ZL)]

    barrier = pltpu.get_barrier_semaphore()
    peers = [sib] + chips[1:] + [down_same, up_same, up_beside, down_beside, across] + zs[1:]
    for peer in peers:
        pl.semaphore_signal(barrier, inc=1, device_id=peer, device_id_type=MESH)

    loads = [
        pltpu.make_async_copy(og, og_v, lsem.at[0]),
        pltpu.make_async_copy(qw, w2.at[:, 0], lsem.at[1]),
        pltpu.make_async_copy(pw, pw2.at[0], lsem.at[2]),
        pltpu.make_async_copy(pb.at[0], pb2.at[0], lsem.at[3]),
        pltpu.make_async_copy(act, act_v, lsem.at[4]),
    ]
    for load in loads:
        load.start()

    count = [0]

    def remote(src, dst, peer):
        i = count[0]
        count[0] += 1
        return pltpu.make_async_remote_copy(
            src_ref=src,
            dst_ref=dst,
            send_sem=ssem.at[i],
            recv_sem=rsem.at[i],
            device_id=peer,
            device_id_type=MESH,
        )

    started = []

    def go(copy):
        copy.start()
        started.append(copy)
        return copy

    low = lax.broadcasted_iota(jnp.int32, (1, 128), 1) < HD

    loads[0].wait()
    for l in range(LON):
        both = og_v[l].astype(F32)
        pf[CELLS * l : CELLS * (l + 1), :] = jnp.concatenate([both[:, 0], both[:, 1]], axis=1)
    psend[...] = pf[...].astype(BF)

    pl.semaphore_wait(barrier, len(peers))

    p_copy = go(remote(psend, precv, sib))
    for load in loads[1:4]:
        load.wait()
    w_copy = go(remote(w2.at[:, 0], w2.at[:, 1], sib))
    pw_copy = go(remote(pw2.at[0], pw2.at[1], sib))
    pb_copy = go(remote(pb2.at[0], pb2.at[1], sib))

    loads[4].wait()

    def row_of(l):
        both = act_v[l].astype(F32)
        return jnp.where(core == 0, both[:, 0], both[:, 1])

    for l in range(6):
        hs[CELLS * l : CELLS * (l + 1), :] = row_of(l)
    hs[HALF:HPAD, :] = jnp.zeros((HPAD - HALF, D), F32)
    hsend[...] = hs[...].astype(BF)
    plain = lax.div(z + ZL - 1, ZL)
    h_peer = {"lon": down, "tp": beside_tp + (tp - beside_tp) * plain}
    h_copy = go(remote(hsend, hrecv, h_peer))

    p_copy.wait_recv()
    mine = low == (core == 0)
    merged = jnp.where(mine, pf[...], pltpu.roll(precv[...].astype(F32), HD, 1))
    town[...] = merged[0:HPAD]
    tsend[...] = merged[0:HPAD].astype(BF)
    t_copy = go(remote(tsend, trecv, down_same))
    tsh[0 : NT - HALF, :] = merged[HALF:NT]
    g[0, chip] = merged[HALF : HALF + WT].astype(BF)
    ag = [[], []]
    for k in range(1, CHIPS):
        ag[0].append(go(remote(g.at[0, chip], g.at[0, chip], chips[k])))

    for l in range(6, LON):
        xs[CELLS * (l - 6) : CELLS * (l - 5), :] = row_of(l)

    def norm(w):
        def body(i, carry):
            r = pl.ds(pl.multiple_of(WT * w + 48 * i, 16), 48)
            x = xs[r, :]
            cen = x - jnp.mean(x, axis=1, keepdims=True)
            inv = lax.rsqrt(jnp.mean(cen * cen, axis=1, keepdims=True) + 1e-05)
            y = cen * inv
            nf[r, :] = y
            xb[r, :] = y.astype(BF)
            inv_s[r, :] = jnp.broadcast_to(inv, (48, 128))
            return carry

        lax.fori_loop(0, 3, body, 0)

    t_copy.wait_recv()
    tsh[NT - HALF : NT, :] = trecv[...].astype(F32)[0:HALF]
    g[1, chip] = tsh[WT:NT, :].astype(BF)
    for k in range(1, CHIPS):
        ag[1].append(go(remote(g.at[1, chip], g.at[1, chip], chips[k])))

    norm(0)
    w_copy.wait_recv()
    pw_copy.wait_recv()
    pb_copy.wait_recv()

    def weights():
        return w2[...].reshape(6 * HD, D)

    wsum = nt(jnp.ones((8, D), BF), weights())[0:1]

    def forward(w):
        r = pl.ds(WT * w, WT)
        qkv = nt(xb[r, :], weights()).astype(BF)
        qkv_s[r, :] = qkv
        q2, k2, v2 = qkv[:, 0:128], qkv[:, 128:256], qkv[:, 256:384]
        att = []
        for h in range(2):
            keep = low if h == 0 else jnp.logical_not(low)
            s = nt(jnp.where(keep, q2, jnp.zeros_like(q2)), k2) * SCALE + pb2[h]
            e = jnp.exp(s - jnp.max(s, axis=1, keepdims=True))
            p = e * (1.0 / jnp.sum(e, axis=1, keepdims=True))
            probs_s[w, h] = p
            att.append(nn(p.astype(BF), v2))
        att_s[r, :] = jnp.where(low, att[0], att[1]).astype(BF)

    forward(0)


    def backward(w):
        r = pl.ds(WT * w, WT)
        grads = jnp.concatenate([g[w, m] for m in range(CHIPS)], axis=1)
        ga = nt(grads, pw2[...].reshape(2 * HD, D)).astype(BF)
        q2, k2, v2 = qkv_s[r, 0:128], qkv_s[r, 128:256], qkv_s[r, 256:384]
        dq, dk, dv = [], [], []
        for h in range(2):
            keep = low if h == 0 else jnp.logical_not(low)
            p = probs_s[w, h]
            gp = nt(jnp.where(keep, ga, jnp.zeros_like(ga)), v2)
            ds = p * (gp - jnp.sum(gp * p, axis=1, keepdims=True))
            if w == 0:
                b_own[h] = ds
            else:
                b_own[h] = b_own[h] + ds
            dl = ds.astype(BF)
            dv.append(tn(p.astype(BF), ga))
            dq.append(nn(dl, k2) * SCALE)
            dk.append(tn(dl, q2) * SCALE)
        dqkv_s[r, 0:128] = jnp.where(low, dq[0], dq[1]).astype(BF)
        dqkv_s[r, 128:256] = jnp.where(low, dk[0], dk[1]).astype(BF)
        dqkv_s[r, 256:384] = jnp.where(low, dv[0], dv[1]).astype(BF)

    early, late, rest = (0, 0, 80), (0, 80, 64), (1, 0, 80)
    rs = {}
    over = pl.ds(WT - HPAD, HPAD)

    def send_out(part):
        w, a, n = part
        rows = pl.ds(a, n)
        rs[part] = []
        for k in range(1, 4):
            to = lax.rem(row + k, 4)
            rs[part].append(
                go(remote(rs_send.at[w, to, :, rows], rs_recv.at[w, k - 1, :, rows], ys[k]))
            )

    def input_grad(w):
        r = pl.ds(WT * w, WT)
        dq = dqkv_s[r, :]
        wide = dq.astype(F32)
        inv = inv_s[r, 0:1]
        first = jnp.sum(wide * wsum, axis=1, keepdims=True) * (1.0 / D)
        second = jnp.sum(wide * qkv_s[r, :].astype(F32), axis=1, keepdims=True) * (1.0 / D)
        for m in range(CHIPS):
            lanes = slice(128 * m, 128 * (m + 1))
            part = nn(dq, w2[:, :, :, lanes].reshape(6 * HD, 128))
            part = inv * (part - first - nf[r, lanes] * second)
            rs_send[w, m // 2, m % 2] = part.astype(BF)

    for copy in ag[0]:
        copy.wait_recv()
    backward(0)
    input_grad(0)

    h_copy.wait_recv()
    xs[NT - HALF : NT, :] = hrecv[...].astype(F32)[0:HALF]
    norm(1)
    forward(1)

    for copy in ag[1]:
        copy.wait_recv()
    send_out(late)

    def weight_grad(parts, own, send):
        for m in range(CHIPS):
            for i, c in enumerate(parts):
                if c < 3:
                    left, right = dqkv_s[:, 128 * c : 128 * (c + 1)], xb[:, 128 * m : 128 * (m + 1)]
                else:
                    left = att_s[...]
                    right = jnp.concatenate([g[0, m], g[1, m]], axis=0)
                part = tn(left, right)
                own[m, HD * i : HD * (i + 1), :] = part[0:HD]
                send[m, HD * i : HD * (i + 1), :] = part[HD:128].astype(BF)

    weight_grad((3,), mp_own, mp_send)
    mp_copy = go(remote(mp_send, mp_recv, sib))
    backward(1)

    input_grad(1)
    halo_copies = []
    for k in range(1, 4):
        to = lax.rem(row + k, 4)
        halo_copies.append(go(remote(rs_send.at[1, to, :, over], hr_recv.at[k - 1], ys[k])))
    b_send[:, 0:WT] = b_own[1].astype(BF)
    b_copy = go(remote(b_send, b_recv, sib))
    weight_grad((0, 2), ma_own, ma_send)
    far = (1 - xh) * 4
    near = xh * 4
    ma_copies = [
        go(remote(ma_send.at[pl.ds(i, 4)], ma_recv.at[pl.ds(i, 4)], sib)) for i in (far, near)
    ]

    def packed(total):
        top, bottom = total[0:HD], total[HD:128]
        return (
            jnp.where(low, top, pltpu.roll(bottom, HD, 1)),
            jnp.where(low, pltpu.roll(top, HD, 1), bottom),
        )

    def start_z(copy, own, recv, z_own, z_send, z_recv):
        copy.wait_recv()
        for m in range(4):
            first = own[m] + recv[m].astype(F32)
            second = own[m + 4] + recv[m + 4].astype(F32)
            even = jnp.where(low, first, pltpu.roll(second, HD, 1))
            odd = jnp.where(low, pltpu.roll(first, HD, 1), second)
            z_own[2 * m] = even
            z_own[2 * m + 1] = odd
            z_send[2 * m] = even.astype(BF)
            z_send[2 * m + 1] = odd.astype(BF)
        out = []
        for k in range(1, ZL):
            to = lax.rem(z + k, ZL)
            out.append(go(remote(z_send.at[to], z_recv.at[k - 1], zs[k])))
        return out

    zp_copies = start_z(mp_copy, mp_own, mp_recv, zp_own, zp_send, zp_recv)
    weight_grad((1,), mk_own, mk_send)
    mk_copy = go(remote(mk_send, mk_recv, sib))
    send_out(early)
    send_out(rest)

    ma_copies[0].wait_recv()
    for j in range(4):
        xa_send[j] = (ma_own[far + j] + ma_recv[far + j].astype(F32)).astype(BF)
    xa_copy = go(remote(xa_send, xa_recv, across))
    zk_copies = start_z(mk_copy, mk_own, mk_recv, zk_own, zk_send, zk_recv)
    b_copy.wait_recv()
    b_own[0] = b_own[0] + b_recv[:, 0:WT].astype(F32)
    half = b_own[0, pl.ds(pl.multiple_of((1 - xh) * HALF, 8), HALF), :]
    bx_send[0:HPAD, :] = jnp.concatenate(
        [half[:, 0:128], jnp.zeros((HPAD - HALF, 128), F32)], axis=0
    ).astype(BF)
    bx_send[HPAD:96, 0:HALF] = half[:, 128:WT].T.astype(BF)
    bx_copy = go(remote(bx_send, bx_recv, across))


    def over_y(part, which):
        w, a, n = part
        rows = slice(a, a + n)
        total = rs_send[w, row, which, rows].astype(F32)
        for k in range(3):
            total = total + rs_recv[w, k, which, rows].astype(F32)
        return total

    def pass_over(part):
        w, a, n = part
        rows = pl.ds(a, n)
        for copy in rs[part]:
            copy.wait_recv()
        rx_send[w, rows] = over_y(part, 1 - side).astype(BF)
        return go(remote(rx_send.at[w, rows], rx_recv.at[w, rows], beside))

    def finish(part, copy):
        w, a, n = part
        r = slice(WT * w + a, WT * w + a + n)
        total = tsh[r, :] + over_y(part, side)
        copy.wait_recv()
        total = total + rx_recv[w, a : a + n].astype(F32)
        fin[r, :] = total
        fsend[r, :] = total.astype(BF)

    rx_late = pass_over(late)
    for copy in halo_copies:
        copy.wait_recv()
    for i, (which, peer) in enumerate([(side, up_same), (1 - side, up_beside)]):
        total = rs_send[1, row, which, over].astype(F32)
        for k in range(3):
            total = total + hr_recv[k, which].astype(F32)
        up_send[i] = total.astype(BF)
    up_copies = [
        go(remote(up_send.at[i], up_recv.at[i], peer)) for i, peer in enumerate((up_same, up_beside))
    ]
    finish(late, rx_late)
    f_copies = []

    ma_copies[1].wait_recv()
    xa_copy.wait_recv()
    for j in range(4):
        even, odd = packed(ma_own[near + j] + ma_recv[near + j].astype(F32) + xa_recv[j].astype(F32))
        za_own[2 * j, 0:HD, :] = even
        za_own[2 * j + 1, 0:HD, :] = odd
    bx_copy.wait_recv()
    half = b_own[0, pl.ds(pl.multiple_of(xh * HALF, 8), HALF), :]
    b_own[1, 0:HALF, 0:128] = half[:, 0:128] + bx_recv[...].astype(F32)[0:HALF]
    b_own[1, 0:HALF, 128:WT] = half[:, 128:WT] + bx_recv[HPAD:96, 0:HALF].astype(F32).T
    for i in range(ZL):
        rows = b_own[1, 9 * i : 9 * (i + 1), :]
        za_own[i, HD : HD + 9, :] = rows[:, 0:128]
        za_own[i, HD + 9 : HD + 16, 0:16] = rows[0:7, 128:144]
        za_own[i, HD + 9 : HD + 11, 16:32] = rows[7:9, 128:144]
    za_send[...] = za_own[...].astype(BF)
    za_copies = []
    for k in range(1, ZL):
        to = lax.rem(z + k, ZL)
        za_copies.append(go(remote(za_send.at[to], za_recv.at[k - 1], zs[k])))

    rx_early = pass_over(early)
    rx_rest = pass_over(rest)
    for copy in up_copies:
        copy.wait_recv()
    moved = up_recv[0].astype(F32) + up_recv[1].astype(F32)
    moved = moved[HPAD - HALF : HPAD] + town[0:HALF]
    fh_send[...] = jnp.concatenate([moved, jnp.zeros((HPAD - HALF, 128), F32)], axis=0).astype(BF)
    f_copies.append(go(remote(fh_send, fh_recv, sib)))
    finish(early, rx_early)
    f_copies.append(go(remote(fsend.at[0:WT], frecv.at[0:WT], sib)))
    finish(rest, rx_rest)
    f_copies.append(go(remote(fsend.at[WT : WT + HPAD], frecv.at[WT : WT + HPAD], sib)))

    def over_z(copies, z_own, z_recv):
        for copy in copies:
            copy.wait_recv()
        total = z_own[z]
        for k in range(ZL - 1):
            total = total + z_recv[k].astype(F32)
        return total, pltpu.roll(total, HD, 1)

    proj_sum, proj_turned = over_z(zp_copies, zp_own, zp_recv)
    key_sum, key_turned = over_z(zk_copies, zk_own, zk_recv)
    ahead = jnp.where(low, key_sum, proj_turned)
    behind = jnp.where(low, key_turned, proj_sum)
    xb_send[...] = jnp.where(xh == 0, behind, ahead).astype(BF)
    xb_copy = go(remote(xb_send, xb_recv, across))
    second_half = jnp.where(xh == 0, ahead, behind)

    for copy in f_copies:
        copy.wait_recv()

    def chosen(x):
        return jnp.where(core == 0, x, pltpu.roll(x, HD, 1))

    here = chosen(jnp.concatenate([moved, fin[0 : NT - HALF, :]], axis=0))
    there = jnp.concatenate([fh_recv[...].astype(F32)[0:HALF], frecv[...].astype(F32)[0 : NT - HALF]], axis=0)
    there = chosen(there)
    out[0:NT, :] = jnp.where(
        low, jnp.where(core == 0, here, there), pltpu.roll(jnp.where(core == 0, there, here), HD, 1)
    )

    xb_copy.wait_recv()
    out[NT : NT + HD, :] = second_half + xb_recv[...].astype(F32)

    for copy in za_copies:
        copy.wait_recv()
    total = za_own[z]
    for k in range(ZL - 1):
        total = total + za_recv[k].astype(F32)
    out[NT + HD : NT + HD + 80, :] = total

    for copy in started:
        copy.wait_send()


def unpack(parts, out_in, out_qkv, out_proj, out_bias):
    for l in range(LON):
        x = parts[CELLS * l : CELLS * (l + 1), :]
        out_in[l] = jnp.stack([x[:, 0:HD], x[:, HD:128]], axis=1).astype(BF)
    key_proj = parts[NT : NT + HD, :]
    query_value = parts[NT + HD : NT + 2 * HD, :].T
    out_qkv[0] = query_value[0:HD]
    out_qkv[1] = key_proj.T[0:HD]
    out_qkv[2] = query_value[HD:128]
    out_proj[...] = pltpu.roll(key_proj, HD, 1)[:, 0:HD]
    at = NT + 2 * HD
    out_bias[:, 0, 0:128] = parts[at : at + 9, :]
    out_bias[0:7, 0, 128:144] = parts[at + 9 : at + 16, 0:16]
    out_bias[7:9, 0, 128:144] = parts[at + 9 : at + 11, 16:32]


def per_device(activations, qkv_weight, proj_weight, pos_bias, out_grad):
    v = pltpu.VMEM
    scratch = [
        v((LON, CELLS, ROWS, D), BF),
        v((LON, CELLS, ROWS, HD), BF),
        v((NT, D), F32),
        v((HPAD, D), F32),
        v((HPAD, D), BF),
        v((HPAD, D), BF),
        v((NT, D), F32),
        v((NT, D), BF),
        v((NT, 128), F32),
        v((NT, 128), F32),
        v((NT, 128), BF),
        v((NT, 128), BF),
        v((NT, 128), F32),
        v((HPAD, 128), F32),
        v((HPAD, 128), BF),
        v((HPAD, 128), BF),
        v((3, 2, HD, D), BF),
        v((2, HD, D), BF),
        v((2, WT, WT), F32),
        v((2, CHIPS, WT, 128), BF),
        v((NT, 384), BF),
        v((2, 2, WT, WT), F32),
        v((NT, 128), BF),
        v((NT, 384), BF),
        v((CHIPS, 128, 128), F32),
        v((CHIPS, 128, 128), BF),
        v((CHIPS, 128, 128), BF),
        v((CHIPS, HD, 128), F32),
        v((CHIPS, HD, 128), BF),
        v((CHIPS, HD, 128), BF),
        v((CHIPS, HD, 128), F32),
        v((CHIPS, HD, 128), BF),
        v((CHIPS, HD, 128), BF),
        v((2, WT, WT), F32),
        v((WT, 256), BF),
        v((WT, 256), BF),
        v((4, 128, 128), BF),
        v((4, 128, 128), BF),
        v((96, 128), BF),
        v((96, 128), BF),
        v((ZL, 80, 128), F32),
        v((ZL, 80, 128), BF),
        v((ZL - 1, 80, 128), BF),
        v((ZL, HD, 128), F32),
        v((ZL, HD, 128), BF),
        v((ZL - 1, HD, 128), BF),
        v((ZL, HD, 128), F32),
        v((ZL, HD, 128), BF),
        v((ZL - 1, HD, 128), BF),
        v((HD, 128), BF),
        v((HD, 128), BF),
        v((2, 4, 2, WT, 128), BF),
        v((2, 3, 2, WT, 128), BF),
        v((2, WT, 128), BF),
        v((2, WT, 128), BF),
        v((NT, 128), F32),
        v((NT, 128), BF),
        v((WT + HPAD, 128), BF),
        v((3, 2, HPAD, 128), BF),
        v((2, HPAD, 128), BF),
        v((2, HPAD, 128), BF),
        v((HPAD, 128), BF),
        v((HPAD, 128), BF),
        pltpu.SemaphoreType.DMA((5,)),
        pltpu.SemaphoreType.DMA((72,)),
        pltpu.SemaphoreType.DMA((72,)),
    ]
    hbm = pl.BlockSpec(memory_space=pl.ANY)
    vmem = pl.BlockSpec(memory_space=pltpu.VMEM)
    shapes = (
        jax.ShapeDtypeStruct((LON, CELLS, ROWS, HD), BF),
        jax.ShapeDtypeStruct((3, HD, HD), F32),
        jax.ShapeDtypeStruct((HD, HD), F32),
        jax.ShapeDtypeStruct((9, 1, WT), F32),
    )
    parts = pl.pallas_call(
        kernel,
        out_shape=jax.ShapeDtypeStruct((NT + HD + 80, 128), F32),
        in_specs=[hbm] * 5,
        out_specs=vmem,
        scratch_shapes=scratch,
        compiler_params=pltpu.CompilerParams(
            collective_id=0, has_side_effects=True, vmem_limit_bytes=60 << 20
        ),
    )(
        activations.transpose(0, 2, 1, 3),
        qkv_weight.transpose(0, 2, 1),
        proj_weight,
        pos_bias,
        out_grad.transpose(0, 2, 1, 3),
    )
    in_grad, qkv_grad, proj_grad, bias_grad = pl.pallas_call(
        unpack,
        out_shape=shapes,
        in_specs=[vmem],
        out_specs=(vmem,) * 4,
        compiler_params=pltpu.CompilerParams(vmem_limit_bytes=60 << 20),
    )(parts)
    return in_grad.transpose(0, 2, 1, 3), qkv_grad, proj_grad, bias_grad.transpose(1, 0, 2)


def solution(mesh):
    placed = (
        P("lon", None, None, None),
        P(None, None, "tp"),
        P("tp", None),
        P("tp", None, None),
        P("lon", None, None, "tp"),
    )
    return jax.shard_map(
        per_device,
        mesh=mesh,
        in_specs=placed,
        out_specs=(
            P("lon", None, None, "tp"),
            P(None, "lon", "tp"),
            P("tp", "lon"),
            P("tp", "lon", None),
        ),
        check_vma=False,
    )
```

```python
import jax
import jax.numpy as jnp
from jax import lax
from jax.experimental import pallas as pl
from jax.experimental.pallas import tpu as pltpu
from jax.sharding import PartitionSpec as P

BF = jnp.bfloat16
F32 = jnp.float32
MESH = pl.DeviceIdType.MESH

LON = 24
ROWS = 2
CELLS = 12
D = 1024
HD = 64
WT = 144
NT = 288
HALF = 72
HPAD = 80
CHIPS = 8
ZL = 8
SCALE = 0.125


def nt(a, b):
    return lax.dot_general(a, b, (((1,), (1,)), ((), ())), preferred_element_type=F32)


def tn(a, b):
    return lax.dot_general(a, b, (((0,), (0,)), ((), ())), preferred_element_type=F32)


def nn(a, b):
    return jnp.dot(a, b, preferred_element_type=F32)


def kernel(
    act,
    qw,
    pw,
    pb,
    og,
    out,
    outv,
    act_v,
    og_v,
    xs,
    hs,
    hsend,
    hrecv,
    nf,
    xb,
    inv_s,
    pf,
    psend,
    precv,
    tsh,
    town,
    trecv,
    w2,
    pw2,
    pb2,
    g,
    qkv_s,
    probs_s,
    att_s,
    dqkv_s,
    ma_own,
    ma_send,
    ma_recv,
    mk_own,
    mk_send,
    mk_recv,
    mp_own,
    mp_send,
    mp_recv,
    b_own,
    b_send,
    b_recv,
    xa_send,
    xa_recv,
    bx_send,
    bx_recv,
    za_own,
    za_send,
    za_recv,
    zk_own,
    zk_send,
    zk_recv,
    zp_own,
    zp_send,
    zp_recv,
    xb_send,
    xb_recv,
    rs_send,
    rs_recv,
    rx_send,
    rx_recv,
    fin,
    fsend,
    frecv,
    hr_recv,
    up_send,
    up_recv,
    fh_send,
    fh_recv,
    lsem,
    ssem,
    rsem,
):
    tp = lax.axis_index("tp")
    lon = lax.axis_index("lon")
    core = lax.rem(tp, 2)
    chip = lax.div(tp, 2)
    xh = lax.div(lon, ZL)
    z = lax.rem(lon, ZL)
    sib_tp = chip * 2 + 1 - core
    up = lax.rem(lon + 1, 16)
    down = lax.rem(lon + 15, 16)
    sib = {"tp": sib_tp}
    down_same = {"lon": down}
    up_same = {"lon": up}
    across = {"lon": (1 - xh) * ZL + z}
    chips = [None] + [{"tp": lax.rem(chip + k, CHIPS) * 2 + core} for k in range(1, CHIPS)]
    row, side = lax.div(chip, 2), lax.rem(chip, 2)
    ys = [None] + [{"tp": (lax.rem(row + k, 4) * 2 + side) * 2 + core} for k in range(1, 4)]
    beside_tp = (row * 2 + 1 - side) * 2 + core
    beside = {"tp": beside_tp}
    up_beside = {"lon": up, "tp": beside_tp}
    down_beside = {"lon": down, "tp": beside_tp}
    up_cross = {"lon": up, "tp": sib_tp}
    down_cross = {"lon": down, "tp": sib_tp}
    zs = [None] + [{"lon": xh * ZL + lax.rem(z + k, ZL)} for k in range(1, ZL)]

    barrier = pltpu.get_barrier_semaphore()
    peers = [down_same, up_same, up_beside, down_beside, up_cross, down_cross, across]
    peers = peers + zs[4:] + zs[1:4] + chips[1:] + [sib]
    for peer in peers:
        pl.semaphore_signal(barrier, inc=1, device_id=peer, device_id_type=MESH)

    loads = [
        pltpu.make_async_copy(og, og_v, lsem.at[0]),
        pltpu.make_async_copy(qw, w2.at[:, 0], lsem.at[1]),
        pltpu.make_async_copy(pw, pw2.at[0], lsem.at[2]),
        pltpu.make_async_copy(pb.at[0], pb2.at[0], lsem.at[3]),
        pltpu.make_async_copy(act, act_v, lsem.at[4]),
    ]
    for load in loads:
        load.start()

    count = [0]

    def remote(src, dst, peer):
        i = count[0]
        count[0] += 1
        return pltpu.make_async_remote_copy(
            src_ref=src,
            dst_ref=dst,
            send_sem=ssem.at[i],
            recv_sem=rsem.at[i],
            device_id=peer,
            device_id_type=MESH,
        )

    started = []

    def go(copy):
        copy.start()
        started.append(copy)
        return copy

    low = lax.broadcasted_iota(jnp.int32, (1, 128), 1) < HD

    loads[0].wait()
    for l in range(LON):
        both = og_v[l].astype(F32)
        pf[CELLS * l : CELLS * (l + 1), :] = jnp.concatenate([both[:, 0], both[:, 1]], axis=1)
    psend[...] = pf[...].astype(BF)

    pl.semaphore_wait(barrier, len(peers))

    p_copy = go(remote(psend, precv, sib))
    first = psend.at[0:HPAD]
    t_copies = [go(remote(first, trecv.at[0], down_same)), go(remote(first, trecv.at[1], down_cross))]
    for load in loads[1:4]:
        load.wait()
    w_copy = go(remote(w2.at[:, 0], w2.at[:, 1], sib))
    pw_copy = go(remote(pw2.at[0], pw2.at[1], sib))
    pb_copy = go(remote(pb2.at[0], pb2.at[1], sib))

    loads[4].wait()

    def row_of(l):
        both = act_v[l].astype(F32)
        return jnp.where(core == 0, both[:, 0], both[:, 1])

    for l in range(6):
        hs[CELLS * l : CELLS * (l + 1), :] = row_of(l)
    hs[HALF:HPAD, :] = jnp.zeros((HPAD - HALF, D), F32)
    hsend[...] = hs[...].astype(BF)
    plain = lax.div(z + ZL - 1, ZL)
    h_peer = {"lon": down, "tp": beside_tp + (tp - beside_tp) * plain}
    h_copy = go(remote(hsend, hrecv, h_peer))

    p_copy.wait_recv()
    mine = low == (core == 0)
    merged = jnp.where(mine, pf[...], pltpu.roll(precv[...].astype(F32), HD, 1))
    town[...] = merged[0:HPAD]
    tsh[0 : NT - HALF, :] = merged[HALF:NT]
    g[0, chip] = merged[HALF : HALF + WT].astype(BF)
    ag = [[], []]
    for k in range(1, CHIPS):
        ag[0].append(go(remote(g.at[0, chip], g.at[0, chip], chips[k])))

    for l in range(6, LON):
        xs[CELLS * (l - 6) : CELLS * (l - 5), :] = row_of(l)

    def norm(w):
        def body(i, carry):
            r = pl.ds(pl.multiple_of(WT * w + 48 * i, 16), 48)
            x = xs[r, :]
            cen = x - jnp.mean(x, axis=1, keepdims=True)
            inv = lax.rsqrt(jnp.mean(cen * cen, axis=1, keepdims=True) + 1e-05)
            y = cen * inv
            nf[r, :] = y
            xb[r, :] = y.astype(BF)
            inv_s[r, :] = jnp.broadcast_to(inv, (48, 128))
            return carry

        lax.fori_loop(0, 3, body, 0)

    for copy in t_copies:
        copy.wait_recv()
    ahead_rows = jnp.where(
        mine, trecv[0].astype(F32), pltpu.roll(trecv[1].astype(F32), HD, 1)
    )
    tsh[NT - HALF : NT, :] = ahead_rows[0:HALF]
    g[1, chip] = tsh[WT:NT, :].astype(BF)
    for k in range(1, CHIPS):
        ag[1].append(go(remote(g.at[1, chip], g.at[1, chip], chips[k])))

    norm(0)
    w_copy.wait_recv()
    pw_copy.wait_recv()
    pb_copy.wait_recv()

    def weights():
        return w2[...].reshape(6 * HD, D)

    wsum = nt(jnp.ones((8, D), BF), weights())[0:1]

    def forward(w):
        r = pl.ds(WT * w, WT)
        qkv = nt(xb[r, :], weights()).astype(BF)
        qkv_s[r, :] = qkv
        q2, k2, v2 = qkv[:, 0:128], qkv[:, 128:256], qkv[:, 256:384]
        att = []
        for h in range(2):
            keep = low if h == 0 else jnp.logical_not(low)
            s = nt(jnp.where(keep, q2, jnp.zeros_like(q2)), k2) * SCALE + pb2[h]
            e = jnp.exp(s - jnp.max(s, axis=1, keepdims=True))
            p = e * (1.0 / jnp.sum(e, axis=1, keepdims=True))
            probs_s[w, h] = p
            att.append(nn(p.astype(BF), v2))
        att_s[r, :] = jnp.where(low, att[0], att[1]).astype(BF)

    forward(0)


    def backward(w):
        r = pl.ds(WT * w, WT)
        grads = jnp.concatenate([g[w, m] for m in range(CHIPS)], axis=1)
        ga = nt(grads, pw2[...].reshape(2 * HD, D)).astype(BF)
        q2, k2, v2 = qkv_s[r, 0:128], qkv_s[r, 128:256], qkv_s[r, 256:384]
        dq, dk, dv = [], [], []
        for h in range(2):
            keep = low if h == 0 else jnp.logical_not(low)
            p = probs_s[w, h]
            gp = nt(jnp.where(keep, ga, jnp.zeros_like(ga)), v2)
            ds = p * (gp - jnp.sum(gp * p, axis=1, keepdims=True))
            if w == 0:
                b_own[h] = ds
            else:
                b_own[h] = b_own[h] + ds
            dl = ds.astype(BF)
            dv.append(tn(p.astype(BF), ga))
            dq.append(nn(dl, k2) * SCALE)
            dk.append(tn(dl, q2) * SCALE)
        dqkv_s[r, 0:128] = jnp.where(low, dq[0], dq[1]).astype(BF)
        dqkv_s[r, 128:256] = jnp.where(low, dk[0], dk[1]).astype(BF)
        dqkv_s[r, 256:384] = jnp.where(low, dv[0], dv[1]).astype(BF)

    early, late, rest = (0, 0, 80), (0, 80, 64), (1, 0, 80)
    rs = {}
    over = pl.ds(WT - HPAD, HPAD)

    def send_out(part):
        w, a, n = part
        rows = pl.ds(a, n)
        rs[part] = []
        for k in range(1, 4):
            to = lax.rem(row + k, 4)
            rs[part].append(
                go(remote(rs_send.at[w, to, :, rows], rs_recv.at[w, k - 1, :, rows], ys[k]))
            )

    def input_grad(w):
        r = pl.ds(WT * w, WT)
        dq = dqkv_s[r, :]
        wide = dq.astype(F32)
        inv = inv_s[r, 0:1]
        first = jnp.sum(wide * wsum, axis=1, keepdims=True) * (1.0 / D)
        second = jnp.sum(wide * qkv_s[r, :].astype(F32), axis=1, keepdims=True) * (1.0 / D)
        for m in range(CHIPS):
            lanes = slice(128 * m, 128 * (m + 1))
            part = nn(dq, w2[:, :, :, lanes].reshape(6 * HD, 128))
            part = inv * (part - first - nf[r, lanes] * second)
            rs_send[w, m // 2, m % 2] = part.astype(BF)

    for copy in ag[0]:
        copy.wait_recv()
    backward(0)
    input_grad(0)

    h_copy.wait_recv()
    xs[NT - HALF : NT, :] = hrecv[...].astype(F32)[0:HALF]
    norm(1)
    forward(1)

    for copy in ag[1]:
        copy.wait_recv()
    send_out(late)

    def weight_grad(parts, own, send):
        for m in range(CHIPS):
            for i, c in enumerate(parts):
                if c < 3:
                    left, right = dqkv_s[:, 128 * c : 128 * (c + 1)], xb[:, 128 * m : 128 * (m + 1)]
                else:
                    left = att_s[...]
                    right = jnp.concatenate([g[0, m], g[1, m]], axis=0)
                part = tn(left, right)
                own[m, HD * i : HD * (i + 1), :] = part[0:HD]
                send[m, HD * i : HD * (i + 1), :] = part[HD:128].astype(BF)

    weight_grad((3,), mp_own, mp_send)
    mp_copy = go(remote(mp_send, mp_recv, sib))
    backward(1)

    input_grad(1)
    halo_copies = []
    for k in range(1, 4):
        to = lax.rem(row + k, 4)
        halo_copies.append(go(remote(rs_send.at[1, to, :, over], hr_recv.at[k - 1], ys[k])))
    b_send[:, 0:WT] = b_own[1].astype(BF)
    b_copy = go(remote(b_send, b_recv, sib))
    weight_grad((0, 2), ma_own, ma_send)
    far = (1 - xh) * 4
    near = xh * 4
    ma_copies = [
        go(remote(ma_send.at[pl.ds(i, 4)], ma_recv.at[pl.ds(i, 4)], sib)) for i in (far, near)
    ]

    def packed(total):
        top, bottom = total[0:HD], total[HD:128]
        return (
            jnp.where(low, top, pltpu.roll(bottom, HD, 1)),
            jnp.where(low, pltpu.roll(top, HD, 1), bottom),
        )

    def start_z(copy, own, recv, z_own, z_send, z_recv):
        copy.wait_recv()
        for m in range(4):
            first = own[m] + recv[m].astype(F32)
            second = own[m + 4] + recv[m + 4].astype(F32)
            even = jnp.where(low, first, pltpu.roll(second, HD, 1))
            odd = jnp.where(low, pltpu.roll(first, HD, 1), second)
            z_own[2 * m] = even
            z_own[2 * m + 1] = odd
            z_send[2 * m] = even.astype(BF)
            z_send[2 * m + 1] = odd.astype(BF)
        out = []
        for k in range(1, ZL):
            to = lax.rem(z + k, ZL)
            out.append(go(remote(z_send.at[to], z_recv.at[k - 1], zs[k])))
        return out

    zp_copies = start_z(mp_copy, mp_own, mp_recv, zp_own, zp_send, zp_recv)
    weight_grad((1,), mk_own, mk_send)
    mk_copy = go(remote(mk_send, mk_recv, sib))
    send_out(early)
    send_out(rest)

    ma_copies[0].wait_recv()
    for j in range(4):
        xa_send[j] = (ma_own[far + j] + ma_recv[far + j].astype(F32)).astype(BF)
    xa_copy = go(remote(xa_send, xa_recv, across))
    zk_copies = start_z(mk_copy, mk_own, mk_recv, zk_own, zk_send, zk_recv)
    b_copy.wait_recv()
    b_own[0] = b_own[0] + b_recv[:, 0:WT].astype(F32)
    half = b_own[0, pl.ds(pl.multiple_of((1 - xh) * HALF, 8), HALF), :]
    bx_send[0:HPAD, :] = jnp.concatenate(
        [half[:, 0:128], jnp.zeros((HPAD - HALF, 128), F32)], axis=0
    ).astype(BF)
    bx_send[HPAD:96, 0:HALF] = half[:, 128:WT].T.astype(BF)
    bx_copy = go(remote(bx_send, bx_recv, across))


    def over_y(part, which):
        w, a, n = part
        rows = slice(a, a + n)
        total = rs_send[w, row, which, rows].astype(F32)
        for k in range(3):
            total = total + rs_recv[w, k, which, rows].astype(F32)
        return total

    def pass_over(part):
        w, a, n = part
        rows = pl.ds(a, n)
        for copy in rs[part]:
            copy.wait_recv()
        rx_send[w, rows] = over_y(part, 1 - side).astype(BF)
        return go(remote(rx_send.at[w, rows], rx_recv.at[w, rows], beside))

    def finish(part, copy):
        w, a, n = part
        r = slice(WT * w + a, WT * w + a + n)
        total = tsh[r, :] + over_y(part, side)
        copy.wait_recv()
        total = total + rx_recv[w, a : a + n].astype(F32)
        fin[r, :] = total
        fsend[r, :] = total.astype(BF)

    rx_late = pass_over(late)
    for copy in halo_copies:
        copy.wait_recv()
    for i, (which, peer) in enumerate([(side, up_same), (1 - side, up_beside)]):
        total = rs_send[1, row, which, over].astype(F32)
        for k in range(3):
            total = total + hr_recv[k, which].astype(F32)
        up_send[i] = total.astype(BF)
    up_copies = [
        go(remote(up_send.at[i], up_recv.at[i], peer)) for i, peer in enumerate((up_same, up_beside))
    ]
    finish(late, rx_late)
    f_copies = []

    ma_copies[1].wait_recv()
    xa_copy.wait_recv()
    for j in range(4):
        even, odd = packed(ma_own[near + j] + ma_recv[near + j].astype(F32) + xa_recv[j].astype(F32))
        za_own[2 * j, 0:HD, :] = even
        za_own[2 * j + 1, 0:HD, :] = odd
    bx_copy.wait_recv()
    half = b_own[0, pl.ds(pl.multiple_of(xh * HALF, 8), HALF), :]
    b_own[1, 0:HALF, 0:128] = half[:, 0:128] + bx_recv[...].astype(F32)[0:HALF]
    b_own[1, 0:HALF, 128:WT] = half[:, 128:WT] + bx_recv[HPAD:96, 0:HALF].astype(F32).T
    for i in range(ZL):
        rows = b_own[1, 9 * i : 9 * (i + 1), :]
        za_own[i, HD : HD + 9, :] = rows[:, 0:128]
        za_own[i, HD + 9 : HD + 16, 0:16] = rows[0:7, 128:144]
        za_own[i, HD + 9 : HD + 11, 16:32] = rows[7:9, 128:144]
    za_send[...] = za_own[...].astype(BF)
    za_copies = []
    for k in range(1, ZL):
        to = lax.rem(z + k, ZL)
        za_copies.append(go(remote(za_send.at[to], za_recv.at[k - 1], zs[k])))

    rx_early = pass_over(early)
    rx_rest = pass_over(rest)
    for copy in up_copies:
        copy.wait_recv()
    moved = up_recv[0].astype(F32) + up_recv[1].astype(F32)
    moved = moved[HPAD - HALF : HPAD] + town[0:HALF]
    fh_send[...] = jnp.concatenate([moved, jnp.zeros((HPAD - HALF, 128), F32)], axis=0).astype(BF)
    f_copies.append(go(remote(fh_send, fh_recv, sib)))
    finish(early, rx_early)
    f_copies.append(go(remote(fsend.at[0:WT], frecv.at[0:WT], sib)))
    finish(rest, rx_rest)
    f_copies.append(go(remote(fsend.at[WT : WT + HPAD], frecv.at[WT : WT + HPAD], sib)))

    def over_z(copies, z_own, z_recv):
        for copy in copies:
            copy.wait_recv()
        total = z_own[z]
        for k in range(ZL - 1):
            total = total + z_recv[k].astype(F32)
        return total, pltpu.roll(total, HD, 1)

    proj_sum, proj_turned = over_z(zp_copies, zp_own, zp_recv)
    key_sum, key_turned = over_z(zk_copies, zk_own, zk_recv)
    ahead = jnp.where(low, key_sum, proj_turned)
    behind = jnp.where(low, key_turned, proj_sum)
    xb_send[...] = jnp.where(xh == 0, behind, ahead).astype(BF)
    xb_copy = go(remote(xb_send, xb_recv, across))
    second_half = jnp.where(xh == 0, ahead, behind)

    for copy in f_copies:
        copy.wait_recv()

    def chosen(x):
        return jnp.where(core == 0, x, pltpu.roll(x, HD, 1))

    here = chosen(jnp.concatenate([moved, fin[0 : NT - HALF, :]], axis=0))
    there = jnp.concatenate([fh_recv[...].astype(F32)[0:HALF], frecv[...].astype(F32)[0 : NT - HALF]], axis=0)
    there = chosen(there)
    outv[0:NT, :] = jnp.where(
        low, jnp.where(core == 0, here, there), pltpu.roll(jnp.where(core == 0, there, here), HD, 1)
    )

    stores = [pltpu.make_async_copy(outv.at[0:NT], out.at[0:NT], lsem.at[0])]
    stores[0].start()
    xb_copy.wait_recv()
    outv[NT : NT + HD, :] = second_half + xb_recv[...].astype(F32)

    for copy in za_copies:
        copy.wait_recv()
    total = za_own[z]
    for k in range(ZL - 1):
        total = total + za_recv[k].astype(F32)
    outv[NT + HD : NT + HD + 80, :] = total
    tail = pl.ds(NT, HD + 80)
    stores.append(pltpu.make_async_copy(outv.at[tail], out.at[tail], lsem.at[1]))
    stores[1].start()
    for store in stores:
        store.wait()

    for copy in started:
        copy.wait_send()


def unpack(parts, out_in, out_qkv, out_proj, out_bias):
    for l in range(LON):
        x = parts[CELLS * l : CELLS * (l + 1), :]
        out_in[l] = jnp.stack([x[:, 0:HD], x[:, HD:128]], axis=1).astype(BF)
    key_proj = parts[NT : NT + HD, :]
    query_value = parts[NT + HD : NT + 2 * HD, :].T
    out_qkv[0] = query_value[0:HD]
    out_qkv[1] = key_proj.T[0:HD]
    out_qkv[2] = query_value[HD:128]
    out_proj[...] = pltpu.roll(key_proj, HD, 1)[:, 0:HD]
    at = NT + 2 * HD
    out_bias[:, 0, 0:128] = parts[at : at + 9, :]
    out_bias[0:7, 0, 128:144] = parts[at + 9 : at + 16, 0:16]
    out_bias[7:9, 0, 128:144] = parts[at + 9 : at + 11, 16:32]


def per_device(activations, qkv_weight, proj_weight, pos_bias, out_grad):
    v = pltpu.VMEM
    scratch = [
        v((NT + HD + 80, 128), F32),
        v((LON, CELLS, ROWS, D), BF),
        v((LON, CELLS, ROWS, HD), BF),
        v((NT, D), F32),
        v((HPAD, D), F32),
        v((HPAD, D), BF),
        v((HPAD, D), BF),
        v((NT, D), F32),
        v((NT, D), BF),
        v((NT, 128), F32),
        v((NT, 128), F32),
        v((NT, 128), BF),
        v((NT, 128), BF),
        v((NT, 128), F32),
        v((HPAD, 128), F32),
        v((2, HPAD, 128), BF),
        v((3, 2, HD, D), BF),
        v((2, HD, D), BF),
        v((2, WT, WT), F32),
        v((2, CHIPS, WT, 128), BF),
        v((NT, 384), BF),
        v((2, 2, WT, WT), F32),
        v((NT, 128), BF),
        v((NT, 384), BF),
        v((CHIPS, 128, 128), F32),
        v((CHIPS, 128, 128), BF),
        v((CHIPS, 128, 128), BF),
        v((CHIPS, HD, 128), F32),
        v((CHIPS, HD, 128), BF),
        v((CHIPS, HD, 128), BF),
        v((CHIPS, HD, 128), F32),
        v((CHIPS, HD, 128), BF),
        v((CHIPS, HD, 128), BF),
        v((2, WT, WT), F32),
        v((WT, 256), BF),
        v((WT, 256), BF),
        v((4, 128, 128), BF),
        v((4, 128, 128), BF),
        v((96, 128), BF),
        v((96, 128), BF),
        v((ZL, 80, 128), F32),
        v((ZL, 80, 128), BF),
        v((ZL - 1, 80, 128), BF),
        v((ZL, HD, 128), F32),
        v((ZL, HD, 128), BF),
        v((ZL - 1, HD, 128), BF),
        v((ZL, HD, 128), F32),
        v((ZL, HD, 128), BF),
        v((ZL - 1, HD, 128), BF),
        v((HD, 128), BF),
        v((HD, 128), BF),
        v((2, 4, 2, WT, 128), BF),
        v((2, 3, 2, WT, 128), BF),
        v((2, WT, 128), BF),
        v((2, WT, 128), BF),
        v((NT, 128), F32),
        v((NT, 128), BF),
        v((WT + HPAD, 128), BF),
        v((3, 2, HPAD, 128), BF),
        v((2, HPAD, 128), BF),
        v((2, HPAD, 128), BF),
        v((HPAD, 128), BF),
        v((HPAD, 128), BF),
        pltpu.SemaphoreType.DMA((5,)),
        pltpu.SemaphoreType.DMA((72,)),
        pltpu.SemaphoreType.DMA((72,)),
    ]
    hbm = pl.BlockSpec(memory_space=pl.ANY)
    vmem = pl.BlockSpec(memory_space=pltpu.VMEM)
    shapes = (
        jax.ShapeDtypeStruct((LON, CELLS, ROWS, HD), BF),
        jax.ShapeDtypeStruct((3, HD, HD), F32),
        jax.ShapeDtypeStruct((HD, HD), F32),
        jax.ShapeDtypeStruct((9, 1, WT), F32),
    )
    parts = pl.pallas_call(
        kernel,
        out_shape=jax.ShapeDtypeStruct((NT + HD + 80, 128), F32),
        in_specs=[hbm] * 5,
        out_specs=hbm,
        scratch_shapes=scratch,
        compiler_params=pltpu.CompilerParams(
            collective_id=0, has_side_effects=True, vmem_limit_bytes=60 << 20
        ),
    )(
        activations.transpose(0, 2, 1, 3),
        qkv_weight.transpose(0, 2, 1),
        proj_weight,
        pos_bias,
        out_grad.transpose(0, 2, 1, 3),
    )
    in_grad, qkv_grad, proj_grad, bias_grad = pl.pallas_call(
        unpack,
        out_shape=shapes,
        in_specs=[vmem],
        out_specs=(vmem,) * 4,
        compiler_params=pltpu.CompilerParams(vmem_limit_bytes=60 << 20),
    )(parts)
    return in_grad.transpose(0, 2, 1, 3), qkv_grad, proj_grad, bias_grad.transpose(1, 0, 2)


def solution(mesh):
    placed = (
        P("lon", None, None, None),
        P(None, None, "tp"),
        P("tp", None),
        P("tp", None, None),
        P("lon", None, None, "tp"),
    )
    return jax.shard_map(
        per_device,
        mesh=mesh,
        in_specs=placed,
        out_specs=(
            P("lon", None, None, "tp"),
            P(None, "lon", "tp"),
            P("tp", "lon"),
            P("tp", "lon", None),
        ),
        check_vma=False,
    )
```

```python
import jax
import jax.numpy as jnp
from jax import lax
from jax.experimental import pallas as pl
from jax.experimental.pallas import tpu as pltpu
from jax.sharding import PartitionSpec as P

BF = jnp.bfloat16
F32 = jnp.float32
MESH = pl.DeviceIdType.MESH

LON = 24
ROWS = 2
CELLS = 12
D = 1024
HD = 64
WT = 144
NT = 288
HALF = 72
HPAD = 80
CHIPS = 8
ZL = 8
SCALE = 0.125


def nt(a, b):
    return lax.dot_general(a, b, (((1,), (1,)), ((), ())), preferred_element_type=F32)


def tn(a, b):
    return lax.dot_general(a, b, (((0,), (0,)), ((), ())), preferred_element_type=F32)


def nn(a, b):
    return jnp.dot(a, b, preferred_element_type=F32)


def kernel(
    act,
    qw,
    pw,
    pb,
    og,
    out,
    outv,
    act_v,
    og_v,
    xs,
    hs,
    hsend,
    hrecv,
    nf,
    xb,
    inv_s,
    pf,
    psend,
    precv,
    tsh,
    town,
    trecv,
    w2,
    pw2,
    pb2,
    g,
    qkv_s,
    probs_s,
    att_s,
    dqkv_s,
    ma_own,
    ma_send,
    ma_recv,
    mk_own,
    mk_send,
    mk_recv,
    mp_own,
    mp_send,
    mp_recv,
    b_own,
    b_send,
    b_recv,
    xa_send,
    xa_recv,
    bx_send,
    bx_recv,
    za_own,
    za_send,
    za_recv,
    zk_own,
    zk_send,
    zk_recv,
    zp_own,
    zp_send,
    zp_recv,
    xb_send,
    xb_recv,
    rs_send,
    rs_recv,
    rx_send,
    rx_recv,
    fin,
    fsend,
    frecv,
    hr_recv,
    up_send,
    up_recv,
    fh_send,
    fh_recv,
    lsem,
    ssem,
    rsem,
):
    tp = lax.axis_index("tp")
    lon = lax.axis_index("lon")
    core = lax.rem(tp, 2)
    chip = lax.div(tp, 2)
    xh = lax.div(lon, ZL)
    z = lax.rem(lon, ZL)
    sib_tp = chip * 2 + 1 - core
    up = lax.rem(lon + 1, 16)
    down = lax.rem(lon + 15, 16)
    sib = {"tp": sib_tp}
    down_same = {"lon": down}
    up_same = {"lon": up}
    across = {"lon": (1 - xh) * ZL + z}
    chips = [None] + [{"tp": lax.rem(chip + k, CHIPS) * 2 + core} for k in range(1, CHIPS)]
    row, side = lax.div(chip, 2), lax.rem(chip, 2)
    ys = [None] + [{"tp": (lax.rem(row + k, 4) * 2 + side) * 2 + core} for k in range(1, 4)]
    beside_tp = (row * 2 + 1 - side) * 2 + core
    beside = {"tp": beside_tp}
    up_beside = {"lon": up, "tp": beside_tp}
    down_beside = {"lon": down, "tp": beside_tp}
    up_cross = {"lon": up, "tp": sib_tp}
    down_cross = {"lon": down, "tp": sib_tp}
    zs = [None] + [{"lon": xh * ZL + lax.rem(z + k, ZL)} for k in range(1, ZL)]

    barrier = pltpu.get_barrier_semaphore()
    peers = [down_same, up_same, up_beside, down_beside, up_cross, down_cross, across]
    peers = peers + zs[4:] + zs[1:4] + chips[1:] + [sib]
    for peer in peers:
        pl.semaphore_signal(barrier, inc=1, device_id=peer, device_id_type=MESH)

    loads = [
        pltpu.make_async_copy(og, og_v, lsem.at[0]),
        pltpu.make_async_copy(qw, w2.at[:, 0], lsem.at[1]),
        pltpu.make_async_copy(pw, pw2.at[0], lsem.at[2]),
        pltpu.make_async_copy(pb.at[0], pb2.at[0], lsem.at[3]),
        pltpu.make_async_copy(act, act_v, lsem.at[4]),
    ]
    for load in loads:
        load.start()

    count = [0]

    def remote(src, dst, peer):
        i = count[0]
        count[0] += 1
        return pltpu.make_async_remote_copy(
            src_ref=src,
            dst_ref=dst,
            send_sem=ssem.at[i],
            recv_sem=rsem.at[i],
            device_id=peer,
            device_id_type=MESH,
        )

    started = []

    def go(copy):
        copy.start()
        started.append(copy)
        return copy

    low = lax.broadcasted_iota(jnp.int32, (1, 128), 1) < HD

    loads[0].wait()
    for l in range(LON):
        both = og_v[l].astype(F32)
        pf[CELLS * l : CELLS * (l + 1), :] = jnp.concatenate([both[:, 0], both[:, 1]], axis=1)
    psend[...] = pf[...].astype(BF)

    pl.semaphore_wait(barrier, len(peers))

    p_copy = go(remote(psend, precv, sib))
    first = psend.at[0:HPAD]
    t_copies = [go(remote(first, trecv.at[0], down_same)), go(remote(first, trecv.at[1], down_cross))]
    for load in loads[1:4]:
        load.wait()
    w_copy = go(remote(w2.at[:, 0], w2.at[:, 1], sib))
    pw_copy = go(remote(pw2.at[0], pw2.at[1], sib))
    pb_copy = go(remote(pb2.at[0], pb2.at[1], sib))

    loads[4].wait()

    def row_of(l):
        both = act_v[l].astype(F32)
        return jnp.where(core == 0, both[:, 0], both[:, 1])

    for l in range(6):
        hs[CELLS * l : CELLS * (l + 1), :] = row_of(l)
    hs[HALF:HPAD, :] = jnp.zeros((HPAD - HALF, D), F32)
    hsend[...] = hs[...].astype(BF)
    plain = lax.div(z + ZL - 1, ZL)
    h_peer = {"lon": down, "tp": beside_tp + (tp - beside_tp) * plain}
    h_copy = go(remote(hsend, hrecv, h_peer))

    p_copy.wait_recv()
    mine = low == (core == 0)
    merged = jnp.where(mine, pf[...], pltpu.roll(precv[...].astype(F32), HD, 1))
    town[...] = merged[0:HPAD]
    tsh[0 : NT - HALF, :] = merged[HALF:NT]
    g[0, chip] = merged[HALF : HALF + WT].astype(BF)
    ag = [[], []]
    for k in range(1, CHIPS):
        ag[0].append(go(remote(g.at[0, chip], g.at[0, chip], chips[k])))

    for l in range(6, LON):
        xs[CELLS * (l - 6) : CELLS * (l - 5), :] = row_of(l)

    def norm(w):
        def body(i, carry):
            r = pl.ds(pl.multiple_of(WT * w + 48 * i, 16), 48)
            x = xs[r, :]
            cen = x - jnp.mean(x, axis=1, keepdims=True)
            inv = lax.rsqrt(jnp.mean(cen * cen, axis=1, keepdims=True) + 1e-05)
            y = cen * inv
            nf[r, :] = y
            xb[r, :] = y.astype(BF)
            inv_s[r, :] = jnp.broadcast_to(inv, (48, 128))
            return carry

        lax.fori_loop(0, 3, body, 0)

    for copy in t_copies:
        copy.wait_recv()
    ahead_rows = jnp.where(
        mine, trecv[0].astype(F32), pltpu.roll(trecv[1].astype(F32), HD, 1)
    )
    tsh[NT - HALF : NT, :] = ahead_rows[0:HALF]
    g[1, chip] = tsh[WT:NT, :].astype(BF)
    for k in range(1, CHIPS):
        ag[1].append(go(remote(g.at[1, chip], g.at[1, chip], chips[k])))

    norm(0)
    w_copy.wait_recv()
    pw_copy.wait_recv()
    pb_copy.wait_recv()

    def weights():
        return w2[...].reshape(6 * HD, D)

    wsum = nt(jnp.ones((8, D), BF), weights())[0:1]

    def forward(w):
        r = pl.ds(WT * w, WT)
        qkv = nt(xb[r, :], weights()).astype(BF)
        qkv_s[r, :] = qkv
        q2, k2, v2 = qkv[:, 0:128], qkv[:, 128:256], qkv[:, 256:384]
        att = []
        for h in range(2):
            keep = low if h == 0 else jnp.logical_not(low)
            s = nt(jnp.where(keep, q2, jnp.zeros_like(q2)), k2) * SCALE + pb2[h]
            e = jnp.exp(s - jnp.max(s, axis=1, keepdims=True))
            p = e * (1.0 / jnp.sum(e, axis=1, keepdims=True))
            probs_s[w, h] = p
            att.append(nn(p.astype(BF), v2))
        att_s[r, :] = jnp.where(low, att[0], att[1]).astype(BF)

    forward(0)


    def backward(w):
        r = pl.ds(WT * w, WT)
        grads = jnp.concatenate([g[w, m] for m in range(CHIPS)], axis=1)
        ga = nt(grads, pw2[...].reshape(2 * HD, D)).astype(BF)
        q2, k2, v2 = qkv_s[r, 0:128], qkv_s[r, 128:256], qkv_s[r, 256:384]
        dq, dk, dv = [], [], []
        for h in range(2):
            keep = low if h == 0 else jnp.logical_not(low)
            p = probs_s[w, h]
            gp = nt(jnp.where(keep, ga, jnp.zeros_like(ga)), v2)
            ds = p * (gp - jnp.sum(gp * p, axis=1, keepdims=True))
            if w == 0:
                b_own[h] = ds
            else:
                b_own[h] = b_own[h] + ds
            dl = ds.astype(BF)
            dv.append(tn(p.astype(BF), ga))
            dq.append(nn(dl, k2) * SCALE)
            dk.append(tn(dl, q2) * SCALE)
        dqkv_s[r, 0:128] = jnp.where(low, dq[0], dq[1]).astype(BF)
        dqkv_s[r, 128:256] = jnp.where(low, dk[0], dk[1]).astype(BF)
        dqkv_s[r, 256:384] = jnp.where(low, dv[0], dv[1]).astype(BF)

    early, late, rest = (0, 0, 80), (0, 80, 64), (1, 0, 80)
    rs = {}
    over = pl.ds(WT - HPAD, HPAD)

    def send_out(part):
        w, a, n = part
        rows = pl.ds(a, n)
        rs[part] = []
        for k in range(1, 4):
            to = lax.rem(row + k, 4)
            rs[part].append(
                go(remote(rs_send.at[w, to, :, rows], rs_recv.at[w, k - 1, :, rows], ys[k]))
            )

    def input_grad(w):
        r = pl.ds(WT * w, WT)
        dq = dqkv_s[r, :]
        wide = dq.astype(F32)
        inv = inv_s[r, 0:1]
        first = jnp.sum(wide * wsum, axis=1, keepdims=True) * (1.0 / D)
        second = jnp.sum(wide * qkv_s[r, :].astype(F32), axis=1, keepdims=True) * (1.0 / D)
        for m in range(CHIPS):
            lanes = slice(128 * m, 128 * (m + 1))
            part = nn(dq, w2[:, :, :, lanes].reshape(6 * HD, 128))
            part = inv * (part - first - nf[r, lanes] * second)
            rs_send[w, m // 2, m % 2] = part.astype(BF)

    for copy in ag[0]:
        copy.wait_recv()
    backward(0)
    input_grad(0)

    h_copy.wait_recv()
    xs[NT - HALF : NT, :] = hrecv[...].astype(F32)[0:HALF]
    norm(1)
    forward(1)

    for copy in ag[1]:
        copy.wait_recv()
    send_out(late)

    def weight_grad(parts, own, send):
        for m in range(CHIPS):
            for i, c in enumerate(parts):
                if c < 3:
                    left, right = dqkv_s[:, 128 * c : 128 * (c + 1)], xb[:, 128 * m : 128 * (m + 1)]
                else:
                    left = att_s[...]
                    right = jnp.concatenate([g[0, m], g[1, m]], axis=0)
                part = tn(left, right)
                own[m, HD * i : HD * (i + 1), :] = part[0:HD]
                send[m, HD * i : HD * (i + 1), :] = part[HD:128].astype(BF)

    weight_grad((3,), mp_own, mp_send)
    mp_copy = go(remote(mp_send, mp_recv, sib))
    backward(1)

    input_grad(1)
    halo_copies = []
    for k in range(1, 4):
        to = lax.rem(row + k, 4)
        halo_copies.append(go(remote(rs_send.at[1, to, :, over], hr_recv.at[k - 1], ys[k])))
    b_send[:, 0:WT] = b_own[1].astype(BF)
    b_copy = go(remote(b_send, b_recv, sib))
    weight_grad((0, 2), ma_own, ma_send)
    far = (1 - xh) * 4
    near = xh * 4
    ma_copies = [
        go(remote(ma_send.at[pl.ds(i, 4)], ma_recv.at[pl.ds(i, 4)], sib)) for i in (far, near)
    ]

    def packed(total):
        top, bottom = total[0:HD], total[HD:128]
        return (
            jnp.where(low, top, pltpu.roll(bottom, HD, 1)),
            jnp.where(low, pltpu.roll(top, HD, 1), bottom),
        )

    def start_z(copy, own, recv, z_own, z_send, z_recv):
        copy.wait_recv()
        for m in range(4):
            first = own[m] + recv[m].astype(F32)
            second = own[m + 4] + recv[m + 4].astype(F32)
            even = jnp.where(low, first, pltpu.roll(second, HD, 1))
            odd = jnp.where(low, pltpu.roll(first, HD, 1), second)
            z_own[2 * m] = even
            z_own[2 * m + 1] = odd
            z_send[2 * m] = even.astype(BF)
            z_send[2 * m + 1] = odd.astype(BF)
        out = []
        for k in range(1, ZL):
            to = lax.rem(z + k, ZL)
            out.append(go(remote(z_send.at[to], z_recv.at[k - 1], zs[k])))
        return out

    zp_copies = start_z(mp_copy, mp_own, mp_recv, zp_own, zp_send, zp_recv)
    weight_grad((1,), mk_own, mk_send)
    mk_copy = go(remote(mk_send, mk_recv, sib))

    ma_copies[0].wait_recv()
    for j in range(4):
        xa_send[j] = (ma_own[far + j] + ma_recv[far + j].astype(F32)).astype(BF)
    send_out(early)
    send_out(rest)
    xa_copy = go(remote(xa_send, xa_recv, across))
    zk_copies = start_z(mk_copy, mk_own, mk_recv, zk_own, zk_send, zk_recv)
    b_copy.wait_recv()
    b_own[0] = b_own[0] + b_recv[:, 0:WT].astype(F32)
    half = b_own[0, pl.ds(pl.multiple_of((1 - xh) * HALF, 8), HALF), :]
    bx_send[0:HPAD, :] = jnp.concatenate(
        [half[:, 0:128], jnp.zeros((HPAD - HALF, 128), F32)], axis=0
    ).astype(BF)
    bx_send[HPAD:96, 0:HALF] = half[:, 128:WT].T.astype(BF)
    bx_copy = go(remote(bx_send, bx_recv, across))


    def over_y(part, which):
        w, a, n = part
        rows = slice(a, a + n)
        total = rs_send[w, row, which, rows].astype(F32)
        for k in range(3):
            total = total + rs_recv[w, k, which, rows].astype(F32)
        return total

    def pass_over(part):
        w, a, n = part
        rows = pl.ds(a, n)
        for copy in rs[part]:
            copy.wait_recv()
        rx_send[w, rows] = over_y(part, 1 - side).astype(BF)
        return go(remote(rx_send.at[w, rows], rx_recv.at[w, rows], beside))

    def finish(part, copy):
        w, a, n = part
        r = slice(WT * w + a, WT * w + a + n)
        total = tsh[r, :] + over_y(part, side)
        copy.wait_recv()
        total = total + rx_recv[w, a : a + n].astype(F32)
        fin[r, :] = total
        fsend[r, :] = total.astype(BF)

    rx_late = pass_over(late)
    for copy in halo_copies:
        copy.wait_recv()
    for i, (which, peer) in enumerate([(side, up_same), (1 - side, up_beside)]):
        total = rs_send[1, row, which, over].astype(F32)
        for k in range(3):
            total = total + hr_recv[k, which].astype(F32)
        up_send[i] = total.astype(BF)
    up_copies = [
        go(remote(up_send.at[i], up_recv.at[i], peer)) for i, peer in enumerate((up_same, up_beside))
    ]
    finish(late, rx_late)
    f_copies = []

    ma_copies[1].wait_recv()
    xa_copy.wait_recv()
    for j in range(4):
        even, odd = packed(ma_own[near + j] + ma_recv[near + j].astype(F32) + xa_recv[j].astype(F32))
        za_own[2 * j, 0:HD, :] = even
        za_own[2 * j + 1, 0:HD, :] = odd
    bx_copy.wait_recv()
    half = b_own[0, pl.ds(pl.multiple_of(xh * HALF, 8), HALF), :]
    b_own[1, 0:HALF, 0:128] = half[:, 0:128] + bx_recv[...].astype(F32)[0:HALF]
    b_own[1, 0:HALF, 128:WT] = half[:, 128:WT] + bx_recv[HPAD:96, 0:HALF].astype(F32).T
    for i in range(ZL):
        rows = b_own[1, 9 * i : 9 * (i + 1), :]
        za_own[i, HD : HD + 9, :] = rows[:, 0:128]
        za_own[i, HD + 9 : HD + 16, 0:16] = rows[0:7, 128:144]
        za_own[i, HD + 9 : HD + 11, 16:32] = rows[7:9, 128:144]
    za_send[...] = za_own[...].astype(BF)
    za_copies = []
    for k in range(1, ZL):
        to = lax.rem(z + k, ZL)
        za_copies.append(go(remote(za_send.at[to], za_recv.at[k - 1], zs[k])))

    rx_early = pass_over(early)
    rx_rest = pass_over(rest)
    for copy in up_copies:
        copy.wait_recv()
    moved = up_recv[0].astype(F32) + up_recv[1].astype(F32)
    moved = moved[HPAD - HALF : HPAD] + town[0:HALF]
    fh_send[...] = jnp.concatenate([moved, jnp.zeros((HPAD - HALF, 128), F32)], axis=0).astype(BF)
    f_copies.append(go(remote(fh_send, fh_recv, sib)))
    finish(early, rx_early)
    f_copies.append(go(remote(fsend.at[0:WT], frecv.at[0:WT], sib)))
    finish(rest, rx_rest)
    f_copies.append(go(remote(fsend.at[WT : WT + HPAD], frecv.at[WT : WT + HPAD], sib)))

    def over_z(copies, z_own, z_recv):
        for copy in copies:
            copy.wait_recv()
        total = z_own[z]
        for k in range(ZL - 1):
            total = total + z_recv[k].astype(F32)
        return total, pltpu.roll(total, HD, 1)

    proj_sum, proj_turned = over_z(zp_copies, zp_own, zp_recv)
    key_sum, key_turned = over_z(zk_copies, zk_own, zk_recv)
    ahead = jnp.where(low, key_sum, proj_turned)
    behind = jnp.where(low, key_turned, proj_sum)
    xb_send[...] = jnp.where(xh == 0, behind, ahead).astype(BF)
    xb_copy = go(remote(xb_send, xb_recv, across))
    second_half = jnp.where(xh == 0, ahead, behind)

    for copy in f_copies:
        copy.wait_recv()

    def chosen(x):
        return jnp.where(core == 0, x, pltpu.roll(x, HD, 1))

    here = chosen(jnp.concatenate([moved, fin[0 : NT - HALF, :]], axis=0))
    there = jnp.concatenate([fh_recv[...].astype(F32)[0:HALF], frecv[...].astype(F32)[0 : NT - HALF]], axis=0)
    there = chosen(there)
    outv[0:NT, :] = jnp.where(
        low, jnp.where(core == 0, here, there), pltpu.roll(jnp.where(core == 0, there, here), HD, 1)
    )

    stores = [pltpu.make_async_copy(outv.at[0:NT], out.at[0:NT], lsem.at[0])]
    stores[0].start()
    xb_copy.wait_recv()
    outv[NT : NT + HD, :] = second_half + xb_recv[...].astype(F32)

    for copy in za_copies:
        copy.wait_recv()
    total = za_own[z]
    for k in range(ZL - 1):
        total = total + za_recv[k].astype(F32)
    outv[NT + HD : NT + HD + 80, :] = total
    tail = pl.ds(NT, HD + 80)
    stores.append(pltpu.make_async_copy(outv.at[tail], out.at[tail], lsem.at[1]))
    stores[1].start()
    for store in stores:
        store.wait()

    for copy in started:
        copy.wait_send()


def unpack(parts, out_in, out_qkv, out_proj, out_bias):
    for l in range(LON):
        x = parts[CELLS * l : CELLS * (l + 1), :]
        out_in[l] = jnp.stack([x[:, 0:HD], x[:, HD:128]], axis=1).astype(BF)
    key_proj = parts[NT : NT + HD, :]
    query_value = parts[NT + HD : NT + 2 * HD, :].T
    out_qkv[0] = query_value[0:HD]
    out_qkv[1] = key_proj.T[0:HD]
    out_qkv[2] = query_value[HD:128]
    out_proj[...] = pltpu.roll(key_proj, HD, 1)[:, 0:HD]
    at = NT + 2 * HD
    out_bias[:, 0, 0:128] = parts[at : at + 9, :]
    out_bias[0:7, 0, 128:144] = parts[at + 9 : at + 16, 0:16]
    out_bias[7:9, 0, 128:144] = parts[at + 9 : at + 11, 16:32]


def per_device(activations, qkv_weight, proj_weight, pos_bias, out_grad):
    v = pltpu.VMEM
    scratch = [
        v((NT + HD + 80, 128), F32),
        v((LON, CELLS, ROWS, D), BF),
        v((LON, CELLS, ROWS, HD), BF),
        v((NT, D), F32),
        v((HPAD, D), F32),
        v((HPAD, D), BF),
        v((HPAD, D), BF),
        v((NT, D), F32),
        v((NT, D), BF),
        v((NT, 128), F32),
        v((NT, 128), F32),
        v((NT, 128), BF),
        v((NT, 128), BF),
        v((NT, 128), F32),
        v((HPAD, 128), F32),
        v((2, HPAD, 128), BF),
        v((3, 2, HD, D), BF),
        v((2, HD, D), BF),
        v((2, WT, WT), F32),
        v((2, CHIPS, WT, 128), BF),
        v((NT, 384), BF),
        v((2, 2, WT, WT), F32),
        v((NT, 128), BF),
        v((NT, 384), BF),
        v((CHIPS, 128, 128), F32),
        v((CHIPS, 128, 128), BF),
        v((CHIPS, 128, 128), BF),
        v((CHIPS, HD, 128), F32),
        v((CHIPS, HD, 128), BF),
        v((CHIPS, HD, 128), BF),
        v((CHIPS, HD, 128), F32),
        v((CHIPS, HD, 128), BF),
        v((CHIPS, HD, 128), BF),
        v((2, WT, WT), F32),
        v((WT, 256), BF),
        v((WT, 256), BF),
        v((4, 128, 128), BF),
        v((4, 128, 128), BF),
        v((96, 128), BF),
        v((96, 128), BF),
        v((ZL, 80, 128), F32),
        v((ZL, 80, 128), BF),
        v((ZL - 1, 80, 128), BF),
        v((ZL, HD, 128), F32),
        v((ZL, HD, 128), BF),
        v((ZL - 1, HD, 128), BF),
        v((ZL, HD, 128), F32),
        v((ZL, HD, 128), BF),
        v((ZL - 1, HD, 128), BF),
        v((HD, 128), BF),
        v((HD, 128), BF),
        v((2, 4, 2, WT, 128), BF),
        v((2, 3, 2, WT, 128), BF),
        v((2, WT, 128), BF),
        v((2, WT, 128), BF),
        v((NT, 128), F32),
        v((NT, 128), BF),
        v((WT + HPAD, 128), BF),
        v((3, 2, HPAD, 128), BF),
        v((2, HPAD, 128), BF),
        v((2, HPAD, 128), BF),
        v((HPAD, 128), BF),
        v((HPAD, 128), BF),
        pltpu.SemaphoreType.DMA((5,)),
        pltpu.SemaphoreType.DMA((72,)),
        pltpu.SemaphoreType.DMA((72,)),
    ]
    hbm = pl.BlockSpec(memory_space=pl.ANY)
    vmem = pl.BlockSpec(memory_space=pltpu.VMEM)
    shapes = (
        jax.ShapeDtypeStruct((LON, CELLS, ROWS, HD), BF),
        jax.ShapeDtypeStruct((3, HD, HD), F32),
        jax.ShapeDtypeStruct((HD, HD), F32),
        jax.ShapeDtypeStruct((9, 1, WT), F32),
    )
    parts = pl.pallas_call(
        kernel,
        out_shape=jax.ShapeDtypeStruct((NT + HD + 80, 128), F32),
        in_specs=[hbm] * 5,
        out_specs=hbm,
        scratch_shapes=scratch,
        compiler_params=pltpu.CompilerParams(
            collective_id=0, has_side_effects=True, vmem_limit_bytes=60 << 20
        ),
    )(
        activations.transpose(0, 2, 1, 3),
        qkv_weight.transpose(0, 2, 1),
        proj_weight,
        pos_bias,
        out_grad.transpose(0, 2, 1, 3),
    )
    in_grad, qkv_grad, proj_grad, bias_grad = pl.pallas_call(
        unpack,
        out_shape=shapes,
        in_specs=[vmem],
        out_specs=(vmem,) * 4,
        compiler_params=pltpu.CompilerParams(vmem_limit_bytes=60 << 20),
    )(parts)
    return in_grad.transpose(0, 2, 1, 3), qkv_grad, proj_grad, bias_grad.transpose(1, 0, 2)


def solution(mesh):
    placed = (
        P("lon", None, None, None),
        P(None, None, "tp"),
        P("tp", None),
        P("tp", None, None),
        P("lon", None, None, "tp"),
    )
    return jax.shard_map(
        per_device,
        mesh=mesh,
        in_specs=placed,
        out_specs=(
            P("lon", None, None, "tp"),
            P(None, "lon", "tp"),
            P("tp", "lon"),
            P("tp", "lon", None),
        ),
        check_vma=False,
    )
```
